256 devices in a mesh: band: 2 (over core), patch: 128 (over z, x, y).
Axes of the slice: x: 4, y: 4, z: 8, core: 2. Of those that a mesh axis runs over, the one named last changes fastest.
Arguments:
- tiles: bfloat16 [2, 8192, 16384], P('band', 'patch'), may hold values from -6 to 6
- psf_coeff: bfloat16 [2, 8192, 5], P('band', 'patch'), may hold values from -4 to 4
- row_taps: bfloat16 [5, 41], replicated, may hold values from -1 to 1
- col_taps: bfloat16 [5, 41], replicated, may hold values from -1 to 1
- target_patch: int32 [2, 8192, 1], P('band', 'patch'), may hold values from 0 to 127; in each aligned block of 64 rows (0 to 63, 64 to 127, ..., all dimensions but the last counted through in order) at most 2 rows name the same one
- offsets: int32 [2, 8192, 2], P('band', 'patch'), may hold values from 0 to 125
- visits: int32 [2, 8192], P('band', 'patch'), may hold values from 1 to 9
- warp_rows: bfloat16 [2, 8192, 512], P('band', 'patch'), may hold values from 0.099609375 to 1
- warp_cols: bfloat16 [2, 8192, 512], P('band', 'patch'), may hold values from 0.099609375 to 1
- det_taps: float32 [9], replicated, may hold values from 0.05 to 0.4
- band_weight: float32 [2], P('band'), may hold values from 0.5 to 2
Outputs:
- coadd: float32 [2, 32768, 256], P('band', 'patch')
- detection: float32 [32768, 256], P('patch')
The draws below stay inside these ranges and needn't reach their ends.
Inputs may be any that keep to these rules, and one draw needn't show every extreme that they name: `target_patch`: the tiles of one band held by one index of patch name any one patch at most 2 times, a bound that some block reaches.
All inputs are finite; a program needn't handle non-finite values.
Results may differ from the reference program's by a relative error of at most 0.0064.
Values may be sent and summed in bfloat16 or wider, within the bound.
A program may use at most 128 MiB of HBM per device.

```python
import math
import jax
import jax.numpy as jnp
import numpy as np
from jax import lax

TILE = 128
TILE_DEV = 64
NBASIS = 5
TAPS = 41
BW = 4
DTAPS = 9
NBAND = 2
PATCH = 256
CAP = 2
TILES = 8192
NR = 32768
N_PATCH = 128


def touch_ends(array, stream_key, low, high):
    index_at = [jax.random.randint(jax.random.fold_in(stream_key, axis), (), 0, length) for axis, length in enumerate(array.shape)]
    longest = array.shape.index(max(array.shape))
    beside = index_at[:longest] + [(index_at[longest] + 1) % array.shape[longest]] + index_at[longest + 1:]
    return array.at[tuple(index_at)].set(low).at[tuple(beside)].set(high)


def levels(rng, shape, cuts, least, largest):
    gain = 1.0
    for axis_at, shards_of in cuts:
        steps = jax.random.uniform(jax.random.fold_in(jax.random.fold_in(rng, 6), axis_at), (shards_of,), jnp.float32, least / len(cuts), largest / len(cuts))
        gain = gain * jnp.repeat(jnp.exp(steps), shape[axis_at] // shards_of).reshape((-1,) + (1,) * (len(shape) - 1 - axis_at))
    return gain


def deal_out(key, own, number, rows, number_of, top, reach, lean):
    order = jax.random.permutation(key, number_of)
    crowded, usual = load_shares(number_of, rows * top, reach, lean, True), load_shares(number_of, rows * top, reach, lean, False)
    places = jnp.arange(number_of)

    def named(sizes, rotation):
        used = int((sizes > 0).sum())
        fixed = max(1, used // 4)
        moved = fixed + (places - fixed + rotation * (used - fixed)) % max(1, number_of - fixed)
        return jnp.zeros((number_of,), jnp.int32).at[order[jnp.where(places < fixed, places, moved)]].set(jnp.asarray(sizes, jnp.int32))

    sizes = jnp.where(number % 4 == 0, named(crowded, number // 4), named(usual, number - number // 4 - 1))
    mixed = jax.random.permutation(jax.random.fold_in(own, 3), number_of)
    source_of, receiver = mixed[0:number_of // 2 * 2:2], mixed[1:number_of // 2 * 2:2]
    slack = jnp.minimum(sizes[source_of] - 1, reach - sizes[receiver]) // 2
    slack = jnp.where((source_of == order[0]) | (receiver == order[0]) | (sizes[receiver] == 0), 0, jnp.maximum(slack, 0))
    moved = jax.random.randint(jax.random.fold_in(own, 4), (number_of // 2,), 0, 1 << 20) % (slack + 1)
    sizes = sizes.at[source_of].add(-moved).at[receiver].add(moved)
    items = jnp.searchsorted(jnp.cumsum(sizes), jnp.arange(rows * top), side="right").astype(jnp.int32)
    grid = items.reshape(top, rows).T
    grid = grid[jax.random.permutation(jax.random.fold_in(own, 1), rows)]
    rotation = jax.random.randint(jax.random.fold_in(own, 2), (rows, 1), 0, top)
    return jnp.take_along_axis(grid, (jnp.arange(top)[None, :] + rotation) % top, axis=1)


def load_shares(count, total, bound, slope, full):
    weights = [(1 << 20) // math.isqrt(grade ** slope) + 1 for grade in range(1, count + 1)]
    largest = bound if full else min(bound, max(-(-total // count), total * weights[0] // sum(weights)))
    least = 1 if total - largest >= count - 1 else 0
    counts, surplus = [largest] + [least] * (count - 1), total - largest - least * (count - 1)
    while surplus > 0:
        free = [i for i in range(1, count) if counts[i] < largest] or [i for i in range(1, count) if counts[i] < bound]
        mass, left = sum([weights[i] for i in free]), surplus
        for i in free:
            addition = min(bound - counts[i], max(1, left * weights[i] // mass), surplus)
            counts[i] = counts[i] + addition
            surplus = surplus - addition
    return np.array(counts)


def gaussian(stream_key, dims, deviation, most, cuts=(), kind=jnp.bfloat16):
    factor_of = levels(stream_key, dims, cuts, -0.22, 0.18) if cuts else 1.0
    array = jax.random.normal(stream_key, dims, jnp.float32) * deviation * factor_of
    return jnp.minimum(jnp.maximum(array, -most), most).astype(kind)


def setup_inputs(seed: int = 0) -> dict:
    splits = jax.random.split(jax.random.key(seed), 12)
    tiles = gaussian(splits[0], (NBAND, TILES, TILE * TILE), 1.0, 6.0, ((0, 2), (1, 128)))
    psf_coeff = gaussian(splits[1], (NBAND, TILES, NBASIS), 1.0, 4.0, ((0, 2), (1, 128)))
    row_taps = gaussian(splits[2], (NBASIS, TAPS), TAPS ** -0.5, 1.0)
    col_taps = gaussian(splits[3], (NBASIS, TAPS), TAPS ** -0.5, 1.0)
    target_patch_keys = jax.random.split(jax.random.fold_in(splits[4], 1), NBAND * TILES // TILE_DEV)
    target_patch_turns = jax.random.permutation(jax.random.fold_in(splits[4], 3), NBAND * TILES // TILE_DEV)
    target_patch = jax.vmap(lambda own, number: deal_out(jax.random.fold_in(splits[4], 2), own, number, TILE_DEV, N_PATCH, 1, CAP, 2))(target_patch_keys, target_patch_turns).reshape((NBAND, TILES, 1))
    offsets = touch_ends(jax.random.randint(splits[5], (NBAND, TILES, 2), 0, PATCH - TILE - BW + 2), jax.random.fold_in(splits[5], 1), 0, (PATCH - TILE - BW + 2) - 1).astype(jnp.int32)
    visits = touch_ends(jax.random.randint(splits[6], (NBAND, TILES), 1, 10), jax.random.fold_in(splits[6], 1), 1, 9).astype(jnp.int32)
    warp_rows = jnp.clip(jnp.exp(math.log(1.0) - 2.306499 * jax.random.uniform(splits[7], (NBAND, TILES, BW * TILE), jnp.float32) ** levels(splits[7], (NBAND, TILES, BW * TILE), ((0, 2), (1, 128)), -0.2, 0.2)), 0.099609375, 1.0).astype(jnp.bfloat16)
    warp_cols = jnp.clip(jnp.exp(math.log(1.0) - 2.306499 * jax.random.uniform(splits[8], (NBAND, TILES, BW * TILE), jnp.float32) ** levels(splits[8], (NBAND, TILES, BW * TILE), ((0, 2), (1, 128)), -0.2, 0.2)), 0.099609375, 1.0).astype(jnp.bfloat16)
    det_taps = jnp.clip(jnp.exp(jax.random.uniform(splits[9], (DTAPS,), jnp.float32, math.log(0.05), math.log(0.4))), 0.05, 0.4)
    band_weight = jnp.clip(jnp.exp(math.log(2.0) - 1.3862944 * jax.random.uniform(splits[10], (NBAND,), jnp.float32) ** levels(splits[10], (NBAND,), ((0, 2),), -0.2, 0.2)), 0.5, 2.0)
    return dict(tiles=tiles, psf_coeff=psf_coeff, row_taps=row_taps, col_taps=col_taps, target_patch=target_patch, offsets=offsets, visits=visits, warp_rows=warp_rows, warp_cols=warp_cols, det_taps=det_taps, band_weight=band_weight)


def band_matrix(taps, edge):
    half_width = (taps.shape[-1] - 1) // 2
    row_index = lax.broadcasted_iota(jnp.int32, (edge, edge), 0)
    col_index = lax.broadcasted_iota(jnp.int32, (edge, edge), 1)
    offset = col_index - row_index + half_width
    inside = (offset >= 0) & (offset < taps.shape[-1])
    picked = jnp.take(taps, jnp.clip(offset, 0, taps.shape[-1] - 1), axis=-1)
    return jnp.where(inside, picked, jnp.zeros_like(picked))


def coadd_band(images, coefficients, targets, offsets, visits, warp_rows, warp_cols, row_matrix, col_matrix):
    extent = TILE + BW - 1

    def place(totals, slot_items):
        numerator, coverage = totals
        tile_image, coefficient, target, offset, visit_count, row_weights, col_weights = slot_items
        partial_value = jnp.einsum('rc,kmc->rkm', tile_image.astype(jnp.float32), col_matrix)
        scaled = partial_value * coefficient.astype(jnp.float32)[None, :, None]
        scaled = lax.optimization_barrier(scaled.astype(jnp.bfloat16)).astype(jnp.float32)
        matched = jnp.einsum('kir,rkc->ic', row_matrix, scaled)
        matched = lax.optimization_barrier(matched.astype(jnp.bfloat16)).astype(jnp.float32)
        col_float = col_weights.astype(jnp.float32)
        row_scaled = visit_count.astype(jnp.float32) * row_weights.astype(jnp.float32)
        row_scaled = lax.optimization_barrier(row_scaled.astype(jnp.bfloat16)).astype(jnp.float32)
        shifted = jnp.zeros((TILE, extent), jnp.float32)
        colsum = jnp.zeros((extent,), jnp.float32)
        rowsum = jnp.zeros((extent,), jnp.float32)
        for tap_index in range(BW):
            shifted = shifted.at[:, tap_index:tap_index + TILE].add(matched * col_float[tap_index][None, :])
            colsum = colsum.at[tap_index:tap_index + TILE].add(col_float[tap_index])
            rowsum = rowsum.at[tap_index:tap_index + TILE].add(row_scaled[tap_index])
        shifted = lax.optimization_barrier(shifted.astype(jnp.bfloat16)).astype(jnp.float32)
        placed = jnp.zeros((extent, extent), jnp.float32)
        for tap_index in range(BW):
            placed = placed.at[tap_index:tap_index + TILE, :].add(row_scaled[tap_index][:, None] * shifted)
        corner = (target.astype(jnp.int32), offset[0].astype(jnp.int32), offset[1].astype(jnp.int32))
        region = lax.dynamic_slice(numerator, corner, (1, extent, extent))
        numerator = lax.dynamic_update_slice(numerator, region + placed[None], corner)
        region = lax.dynamic_slice(coverage, corner, (1, extent, extent))
        coverage = lax.dynamic_update_slice(coverage, region + (rowsum[:, None] * colsum[None, :])[None], corner)
        return (numerator, coverage), None

    empty = jnp.zeros((N_PATCH, PATCH, PATCH), jnp.float32)
    (numerator, coverage), _ = lax.scan(place, (empty, empty), (images, coefficients, targets, offsets, visits, warp_rows, warp_cols))
    return numerator / jnp.maximum(coverage, 1.0)


def reference(tiles, psf_coeff, row_taps, col_taps, target_patch, offsets, visits, warp_rows, warp_cols, det_taps, band_weight):
    row_matrix = band_matrix(row_taps.astype(jnp.float32), TILE)
    col_matrix = band_matrix(col_taps.astype(jnp.float32), TILE)
    coadd_list = []
    for band_index in range(NBAND):
        images = tiles[band_index].reshape(TILES, TILE, TILE)
        row_weights = warp_rows[band_index].reshape(TILES, BW, TILE)
        col_weights = warp_cols[band_index].reshape(TILES, BW, TILE)
        coadd_image = coadd_band(images, psf_coeff[band_index], target_patch[band_index, :, 0], offsets[band_index], visits[band_index], row_weights, col_weights, row_matrix, col_matrix)
        coadd_list.append(coadd_image.reshape(NR, PATCH))
    coadd = jnp.stack(coadd_list, axis=0)
    combined = jnp.sum(band_weight[:, None, None] * coadd, axis=0)
    half_width = (DTAPS - 1) // 2
    padded = jnp.pad(combined, ((half_width, half_width), (0, 0)))
    row_pass = jnp.zeros((NR, PATCH), jnp.float32)
    for tap_index in range(DTAPS):
        row_pass = row_pass + det_taps[tap_index] * padded[tap_index:tap_index + NR]
    padded = jnp.pad(row_pass, ((0, 0), (half_width, half_width)))
    detection = jnp.zeros((NR, PATCH), jnp.float32)
    for tap_index in range(DTAPS):
        detection = detection + det_taps[tap_index] * padded[:, tap_index:tap_index + PATCH]
    return coadd, detection
```

```python
import functools

import jax
import jax.numpy as jnp
from jax import lax
from jax.experimental import pallas as pl
from jax.experimental.pallas import tpu as pltpu
from jax.sharding import PartitionSpec as P

TILE = 128
BW = 4
PATCH = 256
NTILE = 64
NBASIS = 5
TAPS = 41
NCLASS = 8
CAP = 32
SLOT = 144
WIN = 144
FAC = 16
PROWS = PATCH + FAC
ZROWS = PATCH + 4 * FAC
NZ = 8
MESH = pl.DeviceIdType.MESH
MIB = 1 << 20

bf16, f32, i32 = jnp.bfloat16, jnp.float32, jnp.int32
CONTRACT_LAST = (((1,), (1,)), ((), ()))
CONTRACT_FIRST = (((0,), (0,)), ((), ()))


def coords():
    me = lax.axis_index("patch")
    return me, me // 16, (me // 4) % 4, me % 4


def match_kernel(info, coef, tiles, rtaps, ctaps, wrows, wcols, slots, meta, buf, wr32, wc32, gcat, hstack, counts, sems):
    for k in range(NBASIS):
        for taps, is_row in ((rtaps, True), (ctaps, False)):
            line = taps[k : k + 1, :].astype(f32)
            line = jnp.concatenate([line, jnp.zeros((1, 2 * TILE - TAPS), f32)], axis=1)
            full = jnp.broadcast_to(line, (TILE, 2 * TILE))
            full = pltpu.roll(full, 2 * TILE - (TAPS - 1) // 2, 1)
            full = pltpu.roll(full, 0, 1, stride=1, stride_axis=0)
            band = full[:, :TILE].astype(bf16)
            if is_row:
                gcat[:, k * TILE : (k + 1) * TILE] = band
            else:
                hstack[k * TILE : (k + 1) * TILE, :] = band
    wr32[...] = wrows[...].astype(f32)
    wc32[...] = wcols[...].astype(f32)
    for c in range(NCLASS):
        counts[c] = 0

    def placed(line, offset):
        wide = jnp.concatenate([line, jnp.zeros((BW, TILE), f32)], axis=1)
        wide = jnp.concatenate([wide, jnp.zeros((8 - BW, 2 * TILE), f32)], axis=0)
        summed = jnp.sum(pltpu.roll(wide, 0, 1, stride=1, stride_axis=0), axis=0, keepdims=True)
        return pltpu.roll(summed, offset, 1)

    def tapped(line):
        return jnp.concatenate([line[:, b * TILE : (b + 1) * TILE] for b in range(BW)], axis=0)

    def copy_of(t, position):
        return pltpu.make_async_copy(buf.at[t], slots.at[position], sems.at[t])

    def pair(i, carry):
        images = tiles[pl.ds(2 * i, 2)].reshape(2 * TILE, TILE)
        part = lax.dot_general(images, hstack[...], CONTRACT_LAST, preferred_element_type=f32)
        columns = []
        for u in range(2):
            rows = part[u * TILE : (u + 1) * TILE]
            columns.append(
                jnp.concatenate(
                    [
                        (rows[:, k * TILE : (k + 1) * TILE] * coef[(2 * i + u) * NBASIS + k]).astype(bf16)
                        for k in range(NBASIS)
                    ],
                    axis=0,
                )
            )
        scaled = jnp.concatenate(columns, axis=1)
        matched = jnp.dot(gcat[...], scaled, preferred_element_type=f32).astype(bf16)
        for u in range(2):
            t = 2 * i + u
            target, off_r, off_c, visit = info[t], info[NTILE + t], info[2 * NTILE + t], info[3 * NTILE + t]
            pz, px, py = target // 16, (target // 4) % 4, target % 4
            even = (pz % 2) == 0
            group = jnp.where(even, px, 4 + py)
            inner = jnp.where(even, py, px) * 4 + pz // 2 + jnp.where(even, 0, 16)
            rank = counts[group]
            counts[group] = rank + 1
            meta[group, 0, rank * 4] = inner
            meta[group, 0, rank * 4 + 1] = off_r
            meta[group, 0, rank * 4 + 2] = off_c
            row_line = tapped((wr32[pl.ds(t, 1), :] * visit.astype(f32)).astype(bf16).astype(f32))
            col_line = tapped(wc32[pl.ds(t, 1), :])
            row_sum = placed(row_line, off_r)
            col_sum = placed(col_line, off_c)
            tail = jnp.concatenate(
                [
                    row_line,
                    col_line,
                    row_sum[:, :TILE],
                    row_sum[:, TILE:],
                    col_sum[:, :TILE],
                    col_sum[:, TILE:],
                    jnp.zeros((4, TILE), f32),
                ],
                axis=0,
            )
            buf[t, :TILE, :] = matched[:, u * TILE : (u + 1) * TILE]
            buf[t, TILE:, :] = tail.astype(bf16)
            copy_of(t, group * 32 + rank).start()
        return carry

    lax.fori_loop(0, NTILE // 2, pair, 0)
    for c in range(NCLASS):
        meta[c, 0, 3] = counts[c]

    def finish(t, carry):
        copy_of(t, 0).wait()
        return carry

    lax.fori_loop(0, NTILE, finish, 0)


def match_tiles(info, coef, tiles, rtaps, ctaps, wrows, wcols):
    smem = pl.BlockSpec(memory_space=pltpu.SMEM)
    vmem = pl.BlockSpec(memory_space=pltpu.VMEM)
    return pl.pallas_call(
        match_kernel,
        out_shape=(
            jax.ShapeDtypeStruct((NCLASS * 32, SLOT, TILE), bf16),
            jax.ShapeDtypeStruct((NCLASS, 1, 128), i32),
        ),
        in_specs=[smem, smem] + [vmem] * 5,
        out_specs=(pl.BlockSpec(memory_space=pl.ANY), smem),
        scratch_shapes=[
            pltpu.VMEM((NTILE, SLOT, TILE), bf16),
            pltpu.VMEM((NTILE, BW * TILE), f32),
            pltpu.VMEM((NTILE, BW * TILE), f32),
            pltpu.VMEM((TILE, NBASIS * TILE), bf16),
            pltpu.VMEM((NBASIS * TILE, TILE), bf16),
            pltpu.SMEM((NCLASS,), i32),
            pltpu.SemaphoreType.DMA((NTILE,)),
        ],
        compiler_params=pltpu.CompilerParams(vmem_limit_bytes=40 * MIB),
        name="match",
    )(info, coef, tiles, rtaps, ctaps, wrows, wcols)


def ring_neighbours():
    me, z, x, y = coords()
    return (
        (x, z * 16 + ((x + 1) % 4) * 4 + y, z * 16 + ((x + 3) % 4) * 4 + y),
        (y, z * 16 + x * 4 + (y + 1) % 4, z * 16 + x * 4 + (y + 3) % 4),
    )


def greet(partners):
    barrier = pltpu.get_barrier_semaphore()
    for partner in partners:
        pl.semaphore_signal(barrier, inc=1, device_id=partner, device_id_type=MESH)
    pl.semaphore_wait(barrier, len(partners))


def remote(src, dst, send, recv, patch):
    return pltpu.make_async_remote_copy(
        src_ref=src, dst_ref=dst, send_sem=send, recv_sem=recv, device_id={"patch": patch}, device_id_type=MESH
    )


def ring_exchange(send_block, recv_block, relays, half, size, sends, recvs, first):
    rings = ring_neighbours()
    out, onward = [], []
    n = first
    for a, (here, plus, minus) in enumerate(rings):
        across = (here + 2) % 4
        out.append(remote(send_block(a, across, 0, half), relays.at[2 * a], sends.at[n], recvs.at[n], plus))
        out.append(
            remote(send_block(a, across, half, size - half), relays.at[2 * a + 1], sends.at[n + 1], recvs.at[n + 1], minus)
        )
        n += 2
    for a, (here, plus, minus) in enumerate(rings):
        out.append(
            remote(send_block(a, (here + 1) % 4, 0, size), recv_block(a, here, 0, size), sends.at[n], recvs.at[n], plus)
        )
        out.append(
            remote(send_block(a, (here + 3) % 4, 0, size), recv_block(a, here, 0, size), sends.at[n + 1], recvs.at[n + 1], minus)
        )
        n += 2
    for a, (here, plus, minus) in enumerate(rings):
        onward.append(
            remote(relays.at[2 * a], recv_block(a, (here + 3) % 4, 0, half), sends.at[n], recvs.at[n], plus)
        )
        onward.append(
            remote(relays.at[2 * a + 1], recv_block(a, (here + 1) % 4, half, size - half), sends.at[n + 1], recvs.at[n + 1], minus)
        )
        n += 2
    return out, onward


def route_kernel(cap, slots, meta, recv, rmeta, relays, meta_relays, sends, recvs, local):
    rings = ring_neighbours()
    greet([{"patch": p} for ring in rings for p in ring[1:]])
    own = []
    for a, (here, _, _) in enumerate(rings):
        own.append(pltpu.make_async_copy(slots.at[4 * a + here, pl.ds(0, cap)], recv.at[4 * a + here], local.at[2 * a]))
        own.append(pltpu.make_async_copy(meta.at[4 * a + here], rmeta.at[4 * a + here], local.at[2 * a + 1]))
    mout, monward = [], []
    n = 12
    for a, (here, plus, minus) in enumerate(rings):
        mout.append(remote(meta.at[4 * a + (here + 2) % 4], meta_relays.at[a], sends.at[n], recvs.at[n], plus))
        mout.append(remote(meta.at[4 * a + (here + 1) % 4], rmeta.at[4 * a + here], sends.at[n + 1], recvs.at[n + 1], plus))
        mout.append(remote(meta.at[4 * a + (here + 3) % 4], rmeta.at[4 * a + here], sends.at[n + 2], recvs.at[n + 2], minus))
        monward.append(remote(meta_relays.at[a], rmeta.at[4 * a + (here + 3) % 4], sends.at[n + 3], recvs.at[n + 3], plus))
        n += 4
    out, onward = ring_exchange(
        lambda a, i, start, size: slots.at[4 * a + i, pl.ds(start, size)],
        lambda a, i, start, size: recv.at[4 * a + i, pl.ds(start, size)],
        relays,
        cap // 2,
        cap,
        sends,
        recvs,
        0,
    )
    for copy in mout + out + own:
        copy.start()
    for a in range(2):
        mout[3 * a].wait_recv()
        monward[a].start()
    for i in range(4):
        out[i].wait_recv()
        onward[i].start()
    for i in range(4):
        out[i].wait_send()
    for copy in out[4:]:
        copy.wait()
    for a in range(2):
        mout[3 * a].wait_send()
        mout[3 * a + 1].wait()
        mout[3 * a + 2].wait()
    for copy in monward + onward + own:
        copy.wait()


def route_tiles(slots, meta, cap, collective_id):
    hbm = pl.BlockSpec(memory_space=pl.ANY)
    return pl.pallas_call(
        functools.partial(route_kernel, cap),
        out_shape=(
            jax.ShapeDtypeStruct((NCLASS, cap, SLOT, TILE), bf16),
            jax.ShapeDtypeStruct((NCLASS, 1, 128), i32),
        ),
        in_specs=[hbm, hbm],
        out_specs=(hbm, hbm),
        scratch_shapes=[
            pltpu.VMEM((4, cap // 2, SLOT, TILE), bf16),
            pltpu.VMEM((2, 1, 128), i32),
            pltpu.SemaphoreType.DMA((20,)),
            pltpu.SemaphoreType.DMA((20,)),
            pltpu.SemaphoreType.DMA((4,)),
        ],
        compiler_params=pltpu.CompilerParams(
            collective_id=collective_id, has_side_effects=True, vmem_limit_bytes=40 * MIB
        ),
        name="route",
    )(slots.reshape(NCLASS, 32, SLOT, TILE), meta)


UNROLL = 4


def warp_kernel(cap, meta, recv, out, acc, fac, names, fill):
    acc[...] = jnp.zeros_like(acc)
    fac[...] = jnp.zeros_like(fac)
    for p in range(32):
        fill[p] = 0
    total = jnp.int32(0)
    for c in range(NCLASS):
        here = meta[c, 0, 3]

        def note(s, carry, c=c, total=total):
            names[total + s] = c * cap + s
            return carry

        lax.fori_loop(0, here, note, 0)
        total = total + here
    gap = lax.broadcasted_iota(i32, (PATCH, TILE), 0) - lax.broadcasted_iota(i32, (PATCH, TILE), 1)

    def banded(lines, first, gaps, offset):
        gaps = gaps - offset
        mat = jnp.zeros(gaps.shape, f32)
        for b in range(BW):
            mat = jnp.where(gaps == b, lines[first + b : first + b + 1, :], mat)
        return mat.astype(bf16)

    place = lax.broadcasted_iota(i32, (8, TILE), 0)

    def step(i, carry):
        todo = []
        for u in range(UNROLL):
            n = i * UNROLL + u
            slot = names[jnp.minimum(n, total - 1)]
            group, rank = slot // cap, slot % cap
            inner = meta[group, 0, rank * 4]
            off_r = meta[group, 0, rank * 4 + 1]
            off_c = meta[group, 0, rank * 4 + 2]
            tail = recv[group, rank, TILE:, :].astype(f32)
            live = jnp.where(n < total, 1.0, 0.0).astype(f32)
            colmat = banded(tail, BW, gap, off_c)
            shifted = lax.dot_general(
                recv[group, rank, :TILE, :], colmat, CONTRACT_LAST, preferred_element_type=f32
            ).astype(bf16)
            aligned = pl.multiple_of(jnp.minimum((off_r // 8) * 8, PATCH - WIN), 8)
            rowmat = banded(tail * live, 0, gap[:WIN], off_r - aligned)
            todo.append((n, inner, aligned, tail, jnp.dot(rowmat, shifted, preferred_element_type=f32)))
        for n, inner, aligned, tail, term in todo:
            acc[inner, pl.ds(aligned, WIN), :] += term

            at = fill[inner]
            fill[inner] = at + jnp.where(n < total, 1, 0)
            chosen = jnp.where(n < total, at, FAC)
            for k in range(4):
                rows, lanes = pl.ds(8 * (k // 2), 8), pl.ds(TILE * (k % 2), TILE)
                old = fac[inner, rows, lanes]
                fac[inner, rows, lanes] = jnp.where(place == chosen, tail[8 + k : 9 + k], old)

        return carry

    lax.fori_loop(0, (total + UNROLL - 1) // UNROLL, step, 0)

    def store(p, carry):
        out[p, :PATCH, :] = acc[p].astype(bf16)
        out[p, PATCH:, :] = fac[p].astype(bf16)
        return carry

    lax.fori_loop(0, 32, store, 0)


def warp_tiles(meta, recv, cap):
    return pl.pallas_call(
        functools.partial(warp_kernel, cap),
        out_shape=jax.ShapeDtypeStruct((32, PROWS, PATCH), bf16),
        in_specs=[pl.BlockSpec(memory_space=pltpu.SMEM), pl.BlockSpec(memory_space=pltpu.VMEM)],
        out_specs=pl.BlockSpec(memory_space=pltpu.VMEM),
        scratch_shapes=[
            pltpu.VMEM((32, PATCH, PATCH), f32),
            pltpu.VMEM((32, FAC, PATCH), f32),
            pltpu.SMEM((NCLASS * 32,), i32),
            pltpu.SMEM((32,), i32),
        ],
        compiler_params=pltpu.CompilerParams(vmem_limit_bytes=50 * MIB),
        name="warp",
    )(meta, recv)


def merge_kernel(
    part, taps, weight, coadd, detection, recv, relays, zpart, zrecv, mine, other, halo, rowk, colk, sends, recvs, local
):
    me, z, x, y = coords()
    band = lax.axis_index("band")
    rings = ring_neighbours()
    above, below = (me + 127) % 128, (me + 1) % 128
    partners = [{"patch": p} for ring in rings for p in ring[1:]]
    partners += [{"patch": ((z + d) % NZ) * 16 + x * 4 + y} for d in range(1, NZ)]
    partners += [{"patch": me, "band": 1 - band}]
    partners += [{"patch": p, "band": b} for p in (above, below) for b in (band, 1 - band)]
    greet(partners)
    out, onward = ring_exchange(
        lambda a, i, start, size: part.at[1 - a, i, pl.ds(start, size)],
        lambda a, i, start, size: recv.at[1 - a, i, pl.ds(start, size)],
        relays,
        2,
        4,
        sends,
        recvs,
        0,
    )
    own = [
        pltpu.make_async_copy(part.at[0, y], recv.at[0, y], local.at[0]),
        pltpu.make_async_copy(part.at[1, x], recv.at[1, x], local.at[1]),
    ]
    for copy in out + own:
        copy.start()
    wide = PATCH + 16
    row_gap = lax.broadcasted_iota(i32, (PATCH, wide), 1) - lax.broadcasted_iota(i32, (PATCH, wide), 0) - 4
    col_gap = lax.broadcasted_iota(i32, (PATCH, PATCH), 0) - lax.broadcasted_iota(i32, (PATCH, PATCH), 1) + 4
    row_kernel = jnp.zeros((PATCH, wide), f32)
    col_kernel = jnp.zeros((PATCH, PATCH), f32)
    for r in range(9):
        row_kernel = jnp.where(row_gap == r, taps[r], row_kernel)
        col_kernel = jnp.where(col_gap == r, taps[r], col_kernel)
    rowk[...] = row_kernel
    colk[...] = col_kernel
    for i in range(4):
        out[i].wait_recv()
        onward[i].start()
    for i in range(4):
        out[i].wait_send()
    for copy in out[4:] + onward + own:
        copy.wait()

    for a in range(2):
        def fold(zz, carry, a=a):
            total = jnp.zeros((PATCH, PATCH), f32)
            for s in range(4):
                total = total + recv[a, s, zz, :PATCH, :].astype(f32)
                zpart[2 * zz + a, PATCH + s * FAC : PATCH + (s + 1) * FAC, :] = recv[a, s, zz, PATCH:, :]
            zpart[2 * zz + a, :PATCH, :] = total.astype(bf16)
            return carry

        lax.fori_loop(0, 4, fold, 0)

    zcopies = []
    for d in range(1, NZ):
        to = (z + d) % NZ
        copy = remote(zpart.at[to], zrecv.at[z], sends.at[11 + d], recvs.at[11 + d], to * 16 + x * 4 + y)
        copy.start()
        zcopies.append(copy)
    own = pltpu.make_async_copy(zpart.at[z], zrecv.at[z], local.at[0])
    own.start()
    own.wait()
    for copy in zcopies:
        copy.wait()
    total = jnp.zeros((PATCH, PATCH), f32)
    row_sums, col_sums = [], []
    for s in range(NZ):
        total = total + zrecv[s, :PATCH, :].astype(f32)
        sums = zrecv[s, PATCH:, :].astype(f32)
        for q in range(4):
            row_sums.append(sums[q * FAC : q * FAC + 8])
            col_sums.append(sums[q * FAC + 8 : (q + 1) * FAC])
    cover = lax.dot_general(
        jnp.concatenate(row_sums, axis=0).astype(bf16),
        jnp.concatenate(col_sums, axis=0).astype(bf16),
        CONTRACT_FIRST,
        preferred_element_type=f32,
    )
    image = total / jnp.maximum(cover, 1.0)
    coadd[...] = image
    mine[...] = image * weight[0]

    def to_core(src, dst, n, patch, core):
        return pltpu.make_async_remote_copy(
            src_ref=src,
            dst_ref=dst,
            send_sem=sends.at[n],
            recv_sem=recvs.at[n],
            device_id={"patch": patch, "band": core},
            device_id_type=MESH,
        )

    last = [
        to_core(mine.at[pl.ds(PATCH - 8, 8)], halo.at[0, 0], 19, below, band),
        to_core(mine.at[pl.ds(PATCH - 8, 8)], halo.at[0, 1], 20, below, 1 - band),
        to_core(mine.at[pl.ds(0, 8)], halo.at[1, 0], 21, above, band),
        to_core(mine.at[pl.ds(0, 8)], halo.at[1, 1], 22, above, 1 - band),
        to_core(mine, other, 23, me, 1 - band),
    ]
    for copy in last:
        copy.start()
    for copy in last:
        copy.wait()
    top = jnp.where(me == 0, 0.0, halo[0, 0] + halo[0, 1])
    bottom = jnp.where(me == 127, 0.0, halo[1, 0] + halo[1, 1])
    padded = jnp.concatenate([top, mine[...] + other[...], bottom], axis=0)
    row_pass = jnp.dot(rowk[...], padded, precision=lax.Precision.HIGHEST, preferred_element_type=f32)
    detection[...] = jnp.dot(row_pass, colk[...], precision=lax.Precision.HIGHEST, preferred_element_type=f32)


def merge(part, det_taps, band_weight):
    smem = pl.BlockSpec(memory_space=pltpu.SMEM)
    vmem = pl.BlockSpec(memory_space=pltpu.VMEM)
    image = jax.ShapeDtypeStruct((PATCH, PATCH), f32)
    return pl.pallas_call(
        merge_kernel,
        out_shape=(image, image),
        in_specs=[pl.BlockSpec(memory_space=pl.ANY), smem, smem],
        out_specs=(vmem, vmem),
        scratch_shapes=[
            pltpu.VMEM((2, 4, 4, PROWS, PATCH), bf16),
            pltpu.VMEM((4, 2, PROWS, PATCH), bf16),
            pltpu.VMEM((NZ, ZROWS, PATCH), bf16),
            pltpu.VMEM((NZ, ZROWS, PATCH), bf16),
            pltpu.VMEM((PATCH, PATCH), f32),
            pltpu.VMEM((PATCH, PATCH), f32),
            pltpu.VMEM((2, 2, 8, PATCH), f32),
            pltpu.VMEM((PATCH, PATCH + 16), f32),
            pltpu.VMEM((PATCH, PATCH), f32),
            pltpu.SemaphoreType.DMA((24,)),
            pltpu.SemaphoreType.DMA((24,)),
            pltpu.SemaphoreType.DMA((2,)),
        ],
        compiler_params=pltpu.CompilerParams(collective_id=2, has_side_effects=True, vmem_limit_bytes=50 * MIB),
        name="merge",
    )(part.reshape(2, 4, 4, PROWS, PATCH), det_taps, band_weight)


def body(
    tiles, psf_coeff, row_taps, col_taps, target_patch, offsets, visits, warp_rows, warp_cols, det_taps, band_weight
):
    info = jnp.concatenate([target_patch[0, :, 0], offsets[0, :, 0], offsets[0, :, 1], visits[0]])
    coef = psf_coeff[0].astype(f32).reshape(-1)
    slots, meta = match_tiles(
        info, coef, tiles[0].reshape(NTILE, TILE, TILE), row_taps, col_taps, warp_rows[0], warp_cols[0]
    )
    recv, rmeta = route_tiles(slots, meta, CAP, 0)
    part = warp_tiles(rmeta, recv, CAP)
    coadd, detection = merge(part, det_taps, band_weight)
    return coadd[None], detection


def solution(mesh):
    in_specs = (
        P("band", "patch", None),
        P("band", "patch", None),
        P(),
        P(),
        P("band", "patch", None),
        P("band", "patch", None),
        P("band", "patch"),
        P("band", "patch", None),
        P("band", "patch", None),
        P(),
        P("band"),
    )
    out_specs = (P("band", "patch", None), P("patch", None))
    return jax.shard_map(body, mesh=mesh, in_specs=in_specs, out_specs=out_specs, check_vma=False)
```

```python
import functools

import jax
import jax.numpy as jnp
from jax import lax
from jax.experimental import pallas as pl
from jax.experimental.pallas import tpu as pltpu
from jax.sharding import PartitionSpec as P

TILE = 128
BW = 4
PATCH = 256
NTILE = 64
NBASIS = 5
TAPS = 41
NCLASS = 8
CAP = 16
SLOT = 144
WIN = 144
FAC = 16
PROWS = PATCH + FAC
ZROWS = PATCH + 4 * FAC
NZ = 8
NCHUNK = 4
CHUNK = PATCH // NCHUNK
MESH = pl.DeviceIdType.MESH
MIB = 1 << 20
STEPS = 8

bf16, f32, i32 = jnp.bfloat16, jnp.float32, jnp.int32
CONTRACT_LAST = (((1,), (1,)), ((), ()))
CONTRACT_FIRST = (((0,), (0,)), ((), ()))


def coords():
    me = lax.axis_index("patch")
    return me, me // 16, (me // 4) % 4, me % 4


def match_kernel(
    info, coef, tiles, rtaps, ctaps, wrows, wcols, slots, meta,
    images, rows16, cols16, wr32, wc32, gcat, hstack, counts, places, loads,
):
    chunk = NTILE // STEPS

    def load_of(i):
        part = pl.ds(i * chunk, chunk)
        return pltpu.make_async_copy(tiles.at[part], images.at[part], loads.at[i])

    weights = [
        pltpu.make_async_copy(wrows, rows16, loads.at[STEPS]),
        pltpu.make_async_copy(wcols, cols16, loads.at[STEPS + 1]),
    ]
    for copy in weights + [load_of(i) for i in range(STEPS)]:
        copy.start()
    for k in range(NBASIS):
        for taps, is_row in ((rtaps, True), (ctaps, False)):
            line = taps[k : k + 1, :].astype(f32)
            line = jnp.concatenate([line, jnp.zeros((1, 2 * TILE - TAPS), f32)], axis=1)
            full = jnp.broadcast_to(line, (TILE, 2 * TILE))
            full = pltpu.roll(full, 2 * TILE - (TAPS - 1) // 2, 1)
            full = pltpu.roll(full, 0, 1, stride=1, stride_axis=0)
            band = full[:, :TILE].astype(bf16)
            if is_row:
                gcat[:, k * TILE : (k + 1) * TILE] = band
            else:
                hstack[k * TILE : (k + 1) * TILE, :] = band
    for c in range(NCLASS):
        counts[c] = 0

    def assign(t, carry):
        target = info[t]
        pz, px, py = target // 16, (target // 4) % 4, target % 4
        even = (pz % 2) == 0
        group = jnp.where(even, px, 4 + py)
        rank = counts[group]
        counts[group] = rank + 1
        places[t] = group * 32 + rank
        meta[group, 0, rank * 4] = jnp.where(even, py, px) * 4 + pz // 2 + jnp.where(even, 0, 16)
        meta[group, 0, rank * 4 + 1] = info[NTILE + t]
        meta[group, 0, rank * 4 + 2] = info[2 * NTILE + t]
        return carry

    lax.fori_loop(0, NTILE, assign, 0)
    for c in range(NCLASS):
        meta[c, 0, 3] = counts[c]
    for copy in weights:
        copy.wait()
    wr32[...] = rows16[...].astype(f32)
    wc32[...] = cols16[...].astype(f32)

    def placed(line, offset):
        wide = jnp.concatenate([line, jnp.zeros((BW, TILE), f32)], axis=1)
        wide = jnp.concatenate([wide, jnp.zeros((8 - BW, 2 * TILE), f32)], axis=0)
        summed = jnp.sum(pltpu.roll(wide, 0, 1, stride=1, stride_axis=0), axis=0, keepdims=True)
        return pltpu.roll(summed, offset, 1)

    def tapped(line):
        return jnp.concatenate([line[:, b * TILE : (b + 1) * TILE] for b in range(BW)], axis=0)

    def pack(i, carry):
        for u in range(4):
            t = 4 * i + u
            off_r, off_c, visit = info[NTILE + t], info[2 * NTILE + t], info[3 * NTILE + t]
            row_line = tapped((wr32[pl.ds(t, 1), :] * visit.astype(f32)).astype(bf16).astype(f32))
            col_line = tapped(wc32[pl.ds(t, 1), :])
            row_sum = placed(row_line, off_r)
            col_sum = placed(col_line, off_c)
            tail = [row_line, col_line]
            tail += [row_sum[:, :TILE], row_sum[:, TILE:], col_sum[:, :TILE], col_sum[:, TILE:]]
            tail += [jnp.zeros((4, TILE), f32)]
            slots[places[t], TILE:, :] = jnp.concatenate(tail, axis=0).astype(bf16)
        return carry

    lax.fori_loop(0, NTILE // 4, pack, 0)

    def step(i, carry):
        load_of(i).wait()
        for v in range(chunk // 2):
            first = i * chunk + 2 * v
            pair = images[pl.ds(first, 2)].reshape(2 * TILE, TILE)
            part = lax.dot_general(pair, hstack[...], CONTRACT_LAST, preferred_element_type=f32)
            columns = []
            for u in range(2):
                rows = part[u * TILE : (u + 1) * TILE]
                blocks = [
                    (rows[:, k * TILE : (k + 1) * TILE] * coef[(first + u) * NBASIS + k]).astype(bf16)
                    for k in range(NBASIS)
                ]
                columns.append(jnp.concatenate(blocks, axis=0))
            scaled = jnp.concatenate(columns, axis=1)
            matched = jnp.dot(gcat[...], scaled, preferred_element_type=f32).astype(bf16)
            for u in range(2):
                slots[places[first + u], :TILE, :] = matched[:, u * TILE : (u + 1) * TILE]
        return carry

    lax.fori_loop(0, STEPS, step, 0)


def match_tiles(info, coef, tiles, rtaps, ctaps, wrows, wcols):
    smem = pl.BlockSpec(memory_space=pltpu.SMEM)
    vmem = pl.BlockSpec(memory_space=pltpu.VMEM)
    hbm = pl.BlockSpec(memory_space=pl.ANY)
    return pl.pallas_call(
        match_kernel,
        out_shape=(
            jax.ShapeDtypeStruct((NCLASS * 32, SLOT, TILE), bf16),
            jax.ShapeDtypeStruct((NCLASS, 1, 128), i32),
        ),
        in_specs=[smem, smem, hbm, vmem, vmem, hbm, hbm],
        out_specs=(vmem, smem),
        scratch_shapes=[
            pltpu.VMEM((NTILE, TILE, TILE), bf16),
            pltpu.VMEM((NTILE, BW * TILE), bf16),
            pltpu.VMEM((NTILE, BW * TILE), bf16),
            pltpu.VMEM((NTILE, BW * TILE), f32),
            pltpu.VMEM((NTILE, BW * TILE), f32),
            pltpu.VMEM((TILE, NBASIS * TILE), bf16),
            pltpu.VMEM((NBASIS * TILE, TILE), bf16),
            pltpu.SMEM((NCLASS,), i32),
            pltpu.SMEM((NTILE,), i32),
            pltpu.SemaphoreType.DMA((STEPS + 2,)),
        ],
        compiler_params=pltpu.CompilerParams(vmem_limit_bytes=14 * MIB),
        name="match",
    )(info, coef, tiles, rtaps, ctaps, wrows, wcols)


def greet(partners):
    barrier = pltpu.get_barrier_semaphore()
    for partner in partners:
        pl.semaphore_signal(barrier, inc=1, device_id=partner, device_id_type=MESH)
    pl.semaphore_wait(barrier, len(partners))


def remote(src, dst, send, recv, patch):
    return pltpu.make_async_remote_copy(
        src_ref=src, dst_ref=dst, send_sem=send, recv_sem=recv, device_id={"patch": patch}, device_id_type=MESH
    )


def ring_copies(send_block, recv_block, sends, recvs, first):
    me, z, x, y = coords()
    copies = []
    for d in (2, 1, 3):
        for axis, here in ((0, x), (1, y)):
            there = (here + d) % 4
            owner = z * 16 + there * 4 + y if axis == 0 else z * 16 + x * 4 + there
            n = first + len(copies)
            copies.append(remote(send_block(axis, there), recv_block(axis, here), sends.at[n], recvs.at[n], owner))
    return copies


def ring_partners():
    me, z, x, y = coords()
    partners = [{"patch": z * 16 + ((x + d) % 4) * 4 + y} for d in (1, 2, 3)]
    return partners + [{"patch": z * 16 + x * 4 + (y + d) % 4} for d in (1, 2, 3)]


def column_partners():
    me, z, x, y = coords()
    return [{"patch": ((z + d) % NZ) * 16 + x * 4 + y} for d in range(1, NZ)]


def to_device(src, dst, send, recv, device):
    return pltpu.make_async_remote_copy(
        src_ref=src, dst_ref=dst, send_sem=send, recv_sem=recv, device_id=device, device_id_type=MESH
    )


def route_kernel(cap, slots, meta, recv, rmeta, most, loads, box_x, box_y, box_z, box_b, sends, recvs, local):
    me, z, x, y = coords()
    band = lax.axis_index("band")
    rings, column = ring_partners(), column_partners()
    sibling = {"patch": me, "band": 1 - band}
    greet(rings + column + [sibling])
    small = ring_copies(lambda a, i: meta.at[4 * a + i], lambda a, i: rmeta.at[4 * a + i], sends, recvs, 6)
    for n, own in enumerate((x, 4 + y)):
        small.append(pltpu.make_async_copy(meta.at[own], rmeta.at[own], local.at[n]))
    large = ring_copies(
        lambda a, i: slots.at[4 * a + i, pl.ds(0, cap)], lambda a, i: recv.at[4 * a + i], sends, recvs, 0
    )
    fetch = pltpu.make_async_copy(meta, loads, local.at[2])
    fetch.start()
    for copy in small:
        copy.start()
    fetch.wait()
    top = jnp.max(loads[...], axis=0)
    n = 12
    for box, here, others in (
        (box_x, x, rings[:3]),
        (box_y, y, rings[3:]),
        (box_z, z, column),
        (box_b, band, [sibling]),
    ):
        box[here] = top
        shared = []
        for other in others:
            shared.append(to_device(box.at[here], box.at[here], sends.at[n], recvs.at[n], other))
            n += 1
        for copy in shared:
            copy.start()
        if box is box_y:
            for copy in large:
                copy.start()
        for copy in shared:
            copy.wait()
        top = jnp.max(box[...], axis=0)
    most[...] = top
    for copy in small + large:
        copy.wait()


def route_tiles(slots, meta, cap, collective_id):
    hbm = pl.BlockSpec(memory_space=pl.ANY)
    return pl.pallas_call(
        functools.partial(route_kernel, cap),
        out_shape=(
            jax.ShapeDtypeStruct((NCLASS, cap, SLOT, TILE), bf16),
            jax.ShapeDtypeStruct((NCLASS, 1, 128), i32),
            jax.ShapeDtypeStruct((1, 128), i32),
        ),
        in_specs=[hbm, hbm],
        out_specs=(hbm, hbm, pl.BlockSpec(memory_space=pltpu.VMEM)),
        scratch_shapes=[
            pltpu.VMEM((NCLASS, 1, 128), i32),
            pltpu.VMEM((4, 1, 128), i32),
            pltpu.VMEM((4, 1, 128), i32),
            pltpu.VMEM((NZ, 1, 128), i32),
            pltpu.VMEM((2, 1, 128), i32),
            pltpu.SemaphoreType.DMA((26,)),
            pltpu.SemaphoreType.DMA((26,)),
            pltpu.SemaphoreType.DMA((3,)),
        ],
        compiler_params=pltpu.CompilerParams(
            collective_id=collective_id, has_side_effects=True, vmem_limit_bytes=4 * MIB
        ),
        name="route",
    )(slots.reshape(NCLASS, 32, SLOT, TILE), meta)


UNROLL = 4


def warp_kernel(cap, meta, recv, slots, out, acc, fac, names, fill):
    _, _, x, y = coords()
    for p in range(32):
        fill[p] = 0

    total = jnp.int32(0)
    for c in range(NCLASS):
        here = meta[c, 0, 3]

        def note(s, carry, c=c, total=total):
            names[total + s] = c * 32 + s
            return carry

        lax.fori_loop(0, here, note, 0)
        total = total + here
    acc[...] = jnp.zeros_like(acc)
    fac[...] = jnp.zeros_like(fac)
    gap = lax.broadcasted_iota(i32, (PATCH, TILE), 0) - lax.broadcasted_iota(i32, (PATCH, TILE), 1)

    def banded(lines, first, gaps, offset):
        gaps = gaps - offset
        mat = jnp.zeros(gaps.shape, f32)
        for b in range(BW):
            mat = jnp.where(gaps == b, lines[first + b : first + b + 1, :], mat)
        return mat.astype(bf16)

    place = lax.broadcasted_iota(i32, (8, TILE), 0)

    def step(i, carry):
        todo = []
        for u in range(UNROLL):
            n = i * UNROLL + u
            at = jnp.minimum(n, total - 1)
            slot = names[at]
            group, rank = slot // 32, slot % 32
            inner = meta[group, 0, rank * 4]
            off_r = meta[group, 0, rank * 4 + 1]
            off_c = meta[group, 0, rank * 4 + 2]
            kept = (group == x) | (group == 4 + y)
            image = jnp.where(kept, slots[slot], recv[group, rank])
            tail = image[TILE:, :].astype(f32)
            live = jnp.where(n < total, 1.0, 0.0).astype(f32)
            colmat = banded(tail, BW, gap, off_c)
            shifted = lax.dot_general(
                image[:TILE, :], colmat, CONTRACT_LAST, preferred_element_type=f32
            ).astype(bf16)
            aligned = pl.multiple_of(jnp.minimum((off_r // 8) * 8, PATCH - WIN), 8)
            rowmat = banded(tail * live, 0, gap[:WIN], off_r - aligned)
            todo.append((n, inner, aligned, tail, jnp.dot(rowmat, shifted, preferred_element_type=f32)))
        for n, inner, aligned, tail, term in todo:
            acc[inner, pl.ds(aligned, WIN), :] += term

            at = fill[inner]
            fill[inner] = at + jnp.where(n < total, 1, 0)
            chosen = jnp.where(n < total, at, FAC)
            for k in range(4):
                rows, lanes = pl.ds(8 * (k // 2), 8), pl.ds(TILE * (k % 2), TILE)
                old = fac[inner, rows, lanes]
                fac[inner, rows, lanes] = jnp.where(place == chosen, tail[8 + k : 9 + k], old)

        return carry

    lax.fori_loop(0, (total + UNROLL - 1) // UNROLL, step, 0)

    def store(p, carry):
        out[p, FAC:, :] = acc[p].astype(bf16)
        out[p, :FAC, :] = fac[p].astype(bf16)
        return carry

    lax.fori_loop(0, 32, store, 0)


def warp_tiles(meta, recv, slots, cap):
    vmem = pl.BlockSpec(memory_space=pltpu.VMEM)
    return pl.pallas_call(
        functools.partial(warp_kernel, cap),
        out_shape=jax.ShapeDtypeStruct((32, PROWS, PATCH), bf16),
        in_specs=[pl.BlockSpec(memory_space=pltpu.SMEM), vmem, vmem],
        out_specs=vmem,
        scratch_shapes=[
            pltpu.VMEM((32, PATCH, PATCH), f32),
            pltpu.VMEM((32, FAC, PATCH), f32),
            pltpu.SMEM((NCLASS * 32,), i32),
            pltpu.SMEM((32,), i32),
        ],
        compiler_params=pltpu.CompilerParams(vmem_limit_bytes=18 * MIB),
        name="warp",
    )(meta, recv, slots)


def merge_kernel(
    part, taps, weight, coadd, detection, recv, zpart, zrecv, mine, other, halo, rowk, colk, sends, recvs
):
    me, z, x, y = coords()
    band = lax.axis_index("band")
    above, below = (me + 127) % 128, (me + 1) % 128
    column = column_partners()
    sibling = {"patch": me, "band": 1 - band}
    near = [{"patch": p, "band": b} for p in (above, below) for b in (band, 1 - band)]
    greet(ring_partners() + column + [sibling] + near)

    def rows_of(c, lead):
        start = 0 if c == 0 else lead + c * CHUNK
        return pl.ds(start, lead + CHUNK if c == 0 else CHUNK)

    def ring_part(c):
        rows = rows_of(c, FAC)
        copies = ring_copies(
            lambda a, i: part.at[1 - a, i, pl.ds(0, 4), rows],
            lambda a, i: recv.at[1 - a, i, pl.ds(0, 4), rows],
            sends,
            recvs,
            6 * c,
        )
        for copy in copies:
            copy.start()
        return copies

    pending = [ring_part(0), ring_part(1)]
    wide = PATCH + 16
    row_gap = lax.broadcasted_iota(i32, (PATCH, wide), 1) - lax.broadcasted_iota(i32, (PATCH, wide), 0) - 4
    col_gap = lax.broadcasted_iota(i32, (PATCH, PATCH), 0) - lax.broadcasted_iota(i32, (PATCH, PATCH), 1) + 4
    row_kernel = jnp.zeros((PATCH, wide), f32)
    col_kernel = jnp.zeros((PATCH, PATCH), f32)
    for r in range(9):
        row_kernel = jnp.where(row_gap == r, taps[r], row_kernel)
        col_kernel = jnp.where(col_gap == r, taps[r], col_kernel)
    rowk[...] = row_kernel
    colk[...] = col_kernel

    zcopies = []
    for c in range(NCHUNK):
        for copy in pending[c]:
            copy.wait()
        if c + 2 < NCHUNK:
            pending.append(ring_part(c + 2))
        for a in range(2):

            own = x if a else y

            def fold(zz, carry, a=a, c=c, own=own):
                if c == 0:
                    zpart[2 * zz + a, :FAC, :] = part[a, own, zz, :FAC, :]
                    for d in range(1, 4):
                        zpart[2 * zz + a, d * FAC : (d + 1) * FAC, :] = recv[a, (own + d) % 4, zz, :FAC, :]
                chunk = pl.ds(FAC + c * CHUNK, CHUNK)
                total = part[a, own, zz, chunk, :].astype(f32)
                for d in range(1, 4):
                    total = total + recv[a, (own + d) % 4, zz, chunk, :].astype(f32)
                at = 4 * FAC + c * CHUNK
                zpart[2 * zz + a, at : at + CHUNK, :] = total.astype(bf16)
                return carry

            lax.fori_loop(0, 4, fold, 0)
        rows = rows_of(c, 4 * FAC)
        copies = []
        for d in (4, 3, 5, 2, 6, 1, 7):
            to = (z + d) % NZ
            n = 6 * NCHUNK + 7 * c + d - 1
            copies.append(
                remote(zpart.at[to, rows], zrecv.at[z, rows], sends.at[n], recvs.at[n], to * 16 + x * 4 + y)
            )
        for copy in copies:
            copy.start()
        zcopies.append(copies)

    cover = None
    last = []
    base = 13 * NCHUNK
    for c in range(NCHUNK):
        for copy in zcopies[c]:
            copy.wait()
        if c == 0:
            row_sums, col_sums = [], []
            for d in range(NZ):
                sums = (zrecv[(z + d) % NZ, : 4 * FAC, :] if d else zpart[z, : 4 * FAC, :]).astype(f32)
                for q in range(4):
                    row_sums.append(sums[q * FAC : q * FAC + 8])
                    col_sums.append(sums[q * FAC + 8 : (q + 1) * FAC])
            cover = lax.dot_general(
                jnp.concatenate(row_sums, axis=0).astype(bf16),
                jnp.concatenate(col_sums, axis=0).astype(bf16),
                CONTRACT_FIRST,
                preferred_element_type=f32,
            )
            mine[...] = jnp.maximum(cover, 1.0)
        chunk = pl.ds(4 * FAC + c * CHUNK, CHUNK)
        total = zpart[z, chunk, :].astype(f32)
        for d in range(1, NZ):
            total = total + zrecv[(z + d) % NZ, chunk, :].astype(f32)
        rows = slice(c * CHUNK, (c + 1) * CHUNK)
        image = total / mine[rows, :]
        coadd[rows, :] = image
        mine[rows, :] = image * weight[0]
        ship = pl.ds(c * CHUNK, CHUNK)
        copies = [to_device(mine.at[ship], other.at[ship], sends.at[base + c], recvs.at[base + c], sibling)]
        if c == 0:
            for n in (0, 1):
                k = base + NCHUNK + n
                copies.append(to_device(mine.at[pl.ds(0, 8)], halo.at[1, n], sends.at[k], recvs.at[k], near[n]))
        if c == NCHUNK - 1:
            for n in (0, 1):
                k = base + NCHUNK + 2 + n
                copies.append(
                    to_device(mine.at[pl.ds(PATCH - 8, 8)], halo.at[0, n], sends.at[k], recvs.at[k], near[2 + n])
                )
        for copy in copies:
            copy.start()
        last += copies
    for copy in last:
        copy.wait()
    top = jnp.where(me == 0, 0.0, halo[0, 0] + halo[0, 1])
    bottom = jnp.where(me == 127, 0.0, halo[1, 0] + halo[1, 1])
    padded = jnp.concatenate([top, mine[...] + other[...], bottom], axis=0)
    row_pass = jnp.dot(rowk[...], padded, precision=lax.Precision.HIGHEST, preferred_element_type=f32)
    detection[...] = jnp.dot(row_pass, colk[...], precision=lax.Precision.HIGHEST, preferred_element_type=f32)


def merge(part, det_taps, band_weight):
    smem = pl.BlockSpec(memory_space=pltpu.SMEM)
    vmem = pl.BlockSpec(memory_space=pltpu.VMEM)
    image = jax.ShapeDtypeStruct((PATCH, PATCH), f32)
    count = 14 * NCHUNK + 4
    return pl.pallas_call(
        merge_kernel,
        out_shape=(image, image),
        in_specs=[vmem, smem, smem],
        out_specs=(vmem, vmem),
        scratch_shapes=[
            pltpu.VMEM((2, 4, 4, PROWS, PATCH), bf16),
            pltpu.VMEM((NZ, ZROWS, PATCH), bf16),
            pltpu.VMEM((NZ, ZROWS, PATCH), bf16),
            pltpu.VMEM((PATCH, PATCH), f32),
            pltpu.VMEM((PATCH, PATCH), f32),
            pltpu.VMEM((2, 2, 8, PATCH), f32),
            pltpu.VMEM((PATCH, PATCH + 16), f32),
            pltpu.VMEM((PATCH, PATCH), f32),
            pltpu.SemaphoreType.DMA((count,)),
            pltpu.SemaphoreType.DMA((count,)),
        ],
        compiler_params=pltpu.CompilerParams(collective_id=2, has_side_effects=True, vmem_limit_bytes=14 * MIB),
        name="merge",
    )(part.reshape(2, 4, 4, PROWS, PATCH), det_taps, band_weight)


def body(
    tiles, psf_coeff, row_taps, col_taps, target_patch, offsets, visits, warp_rows, warp_cols, det_taps, band_weight
):
    info = jnp.concatenate([target_patch[0, :, 0], offsets[0, :, 0], offsets[0, :, 1], visits[0]])
    coef = psf_coeff[0].astype(f32).reshape(-1)
    slots, meta = match_tiles(
        info, coef, tiles[0].reshape(NTILE, TILE, TILE), row_taps, col_taps, warp_rows[0], warp_cols[0]
    )
    recv, rmeta, most = route_tiles(slots, meta, CAP, 0)

    def few():
        return warp_tiles(rmeta, recv, slots, CAP)

    def many():
        whole, wmeta, _ = route_tiles(slots, meta, 32, 1)
        return warp_tiles(wmeta, whole, slots, 32)

    part = lax.cond(most[0, 3] > CAP, many, few)
    coadd, detection = merge(part, det_taps, band_weight)
    return coadd[None], detection


def solution(mesh):
    in_specs = (
        P("band", "patch", None),
        P("band", "patch", None),
        P(),
        P(),
        P("band", "patch", None),
        P("band", "patch", None),
        P("band", "patch"),
        P("band", "patch", None),
        P("band", "patch", None),
        P(),
        P("band"),
    )
    out_specs = (P("band", "patch", None), P("patch", None))
    return jax.shard_map(body, mesh=mesh, in_specs=in_specs, out_specs=out_specs, check_vma=False)
```

```python
import functools

import jax
import jax.numpy as jnp
from jax import lax
from jax.experimental import pallas as pl
from jax.experimental.pallas import tpu as pltpu
from jax.sharding import PartitionSpec as P

TILE = 128
BW = 4
PATCH = 256
NTILE = 64
NBASIS = 5
TAPS = 41
NCLASS = 8
CAP = 16
SLOT = 144
WIN = 144
FAC = 16
PROWS = PATCH + FAC
ZROWS = PATCH + 4 * FAC
NZ = 8
NCHUNK = 8
CHUNK = PATCH // NCHUNK
MESH = pl.DeviceIdType.MESH
MIB = 1 << 20
STEPS = 4

bf16, f32, i32 = jnp.bfloat16, jnp.float32, jnp.int32
CONTRACT_LAST = (((1,), (1,)), ((), ()))
CONTRACT_FIRST = (((0,), (0,)), ((), ()))


def coords():
    me = lax.axis_index("patch")
    return me, me // 16, (me // 4) % 4, me % 4


def match_kernel(
    info, packed, tiles, slots, meta, images, coef32, coef, gcat, hstack, wr32, wc32, counts, places, loads
):
    chunk = NTILE // STEPS

    def load_of(i):
        part = pl.ds(i * chunk, chunk)
        return pltpu.make_async_copy(tiles.at[part], images.at[part], loads.at[i])

    for i in range(STEPS):
        load_of(i).start()
    coef32[...] = packed[2 * NTILE : 2 * NTILE + 8, :TILE].astype(f32)
    scalars = pltpu.make_async_copy(coef32, coef, loads.at[STEPS])
    scalars.start()
    wr32[...] = packed[:NTILE, :].astype(f32)
    wc32[...] = packed[NTILE : 2 * NTILE, :].astype(f32)
    for n in range(2):
        first = 2 * NTILE + 16 * (n + 1)
        lines = packed[first : first + 16, : 2 * TILE].astype(f32)
        lines = pltpu.roll(lines, 2 * TILE - (TAPS - 1) // 2, 1)
        for k in range(NBASIS):
            full = jnp.broadcast_to(lines[k : k + 1, :], (TILE, 2 * TILE))
            band = pltpu.roll(full, 0, 1, stride=1, stride_axis=0)[:, :TILE].astype(bf16)
            if n == 0:
                gcat[:, k * TILE : (k + 1) * TILE] = band
            else:
                hstack[k * TILE : (k + 1) * TILE, :] = band
    for c in range(NCLASS):
        counts[c] = 0

    for t in range(NTILE):
        target = info[0, t]
        pz, px, py = target // 16, (target // 4) % 4, target % 4
        even = (pz % 2) == 0
        group = jnp.where(even, px, 4 + py)
        rank = counts[group]
        counts[group] = rank + 1
        places[t] = group * 32 + rank
        meta[group, 0, rank * 4] = jnp.where(even, py, px) * 4 + pz // 2 + jnp.where(even, 0, 16)
        meta[group, 0, rank * 4 + 1] = info[1, t]
        meta[group, 0, rank * 4 + 2] = info[2, t]
    for c in range(NCLASS):
        meta[c, 0, 3] = counts[c]
    def placed(line, offset):
        wide = jnp.concatenate([line, jnp.zeros((BW, TILE), f32)], axis=1)
        wide = jnp.concatenate([wide, jnp.zeros((8 - BW, 2 * TILE), f32)], axis=0)
        summed = jnp.sum(pltpu.roll(wide, 0, 1, stride=1, stride_axis=0), axis=0, keepdims=True)
        return pltpu.roll(summed, offset, 1)

    def tapped(line):
        return jnp.concatenate([line[:, b * TILE : (b + 1) * TILE] for b in range(BW)], axis=0)

    def pack(t):
        off_r, off_c, visit = info[1, t], info[2, t], info[3, t]
        row_line = tapped((wr32[pl.ds(t, 1), :] * visit.astype(f32)).astype(bf16).astype(f32))
        col_line = tapped(wc32[pl.ds(t, 1), :])
        row_sum = placed(row_line, off_r)
        col_sum = placed(col_line, off_c)
        tail = [row_line, col_line]
        tail += [row_sum[:, :TILE], row_sum[:, TILE:], col_sum[:, :TILE], col_sum[:, TILE:]]
        tail += [jnp.zeros((4, TILE), f32)]
        return jnp.concatenate(tail, axis=0).astype(bf16)

    def step(i, carry):
        load_of(i).wait()
        for v in range(chunk // 2):
            first = i * chunk + 2 * v
            pair = images[pl.ds(first, 2)].reshape(2 * TILE, TILE)
            part = lax.dot_general(pair, hstack[...], CONTRACT_LAST, preferred_element_type=f32)
            columns = []
            for u in range(2):
                rows = part[u * TILE : (u + 1) * TILE]
                blocks = [
                    (rows[:, k * TILE : (k + 1) * TILE] * coef[k, first + u]).astype(bf16)
                    for k in range(NBASIS)
                ]
                columns.append(jnp.concatenate(blocks, axis=0))
            scaled = jnp.concatenate(columns, axis=1)
            matched = jnp.dot(gcat[...], scaled, preferred_element_type=f32).astype(bf16)
            for u in range(2):
                at = places[first + u]
                slots[at, :TILE, :] = matched[:, u * TILE : (u + 1) * TILE]
                slots[at, TILE:, :] = pack(first + u)
        return carry

    scalars.wait()
    lax.fori_loop(0, STEPS, step, 0)


def match_tiles(info, packed, tiles):
    smem = pl.BlockSpec(memory_space=pltpu.SMEM)
    vmem = pl.BlockSpec(memory_space=pltpu.VMEM)
    return pl.pallas_call(
        match_kernel,
        out_shape=(
            jax.ShapeDtypeStruct((NCLASS * 32, SLOT, TILE), bf16),
            jax.ShapeDtypeStruct((NCLASS, 1, 128), i32),
        ),
        in_specs=[smem, vmem, pl.BlockSpec(memory_space=pl.ANY)],
        out_specs=(vmem, smem),
        scratch_shapes=[
            pltpu.VMEM((NTILE, TILE, TILE), bf16),
            pltpu.VMEM((8, 128), f32),
            pltpu.SMEM((8, 128), f32),
            pltpu.VMEM((TILE, NBASIS * TILE), bf16),
            pltpu.VMEM((NBASIS * TILE, TILE), bf16),
            pltpu.VMEM((NTILE, BW * TILE), f32),
            pltpu.VMEM((NTILE, BW * TILE), f32),
            pltpu.SMEM((NCLASS,), i32),
            pltpu.SMEM((NTILE,), i32),
            pltpu.SemaphoreType.DMA((STEPS + 1,)),
        ],
        compiler_params=pltpu.CompilerParams(vmem_limit_bytes=24 * MIB),
        name="match",
    )(info, packed, tiles)


def greet(partners):
    barrier = pltpu.get_barrier_semaphore()
    for partner in partners:
        pl.semaphore_signal(barrier, inc=1, device_id=partner, device_id_type=MESH)
    pl.semaphore_wait(barrier, len(partners))


def remote(src, dst, send, recv, patch):
    return pltpu.make_async_remote_copy(
        src_ref=src, dst_ref=dst, send_sem=send, recv_sem=recv, device_id={"patch": patch}, device_id_type=MESH
    )


def ring_copies(send_block, recv_block, sends, recvs, first):
    me, z, x, y = coords()
    copies = []
    for d in (2, 1, 3):
        for axis, here in ((0, x), (1, y)):
            there = (here + d) % 4
            owner = z * 16 + there * 4 + y if axis == 0 else z * 16 + x * 4 + there
            n = first + len(copies)
            copies.append(remote(send_block(axis, there), recv_block(axis, here), sends.at[n], recvs.at[n], owner))
    return copies


def ring_partners():
    me, z, x, y = coords()
    partners = [{"patch": z * 16 + ((x + d) % 4) * 4 + y} for d in (1, 2, 3)]
    return partners + [{"patch": z * 16 + x * 4 + (y + d) % 4} for d in (1, 2, 3)]


def column_partners():
    me, z, x, y = coords()
    return [{"patch": ((z + d) % NZ) * 16 + x * 4 + y} for d in range(1, NZ)]


def to_device(src, dst, send, recv, device):
    return pltpu.make_async_remote_copy(
        src_ref=src, dst_ref=dst, send_sem=send, recv_sem=recv, device_id=device, device_id_type=MESH
    )


def route_kernel(cap, slots, meta, recv, rmeta, most, loads, box_x, box_y, box_z, box_b, sends, recvs, local):
    me, z, x, y = coords()
    band = lax.axis_index("band")
    rings, column = ring_partners(), column_partners()
    sibling = {"patch": me, "band": 1 - band}
    greet(rings + column + [sibling])
    small = ring_copies(lambda a, i: meta.at[4 * a + i], lambda a, i: rmeta.at[4 * a + i], sends, recvs, 6)
    for n, own in enumerate((x, 4 + y)):
        small.append(pltpu.make_async_copy(meta.at[own], rmeta.at[own], local.at[n]))
    large = ring_copies(
        lambda a, i: slots.at[4 * a + i, pl.ds(0, cap)], lambda a, i: recv.at[4 * a + i], sends, recvs, 0
    )
    fetch = pltpu.make_async_copy(meta, loads, local.at[2])
    fetch.start()
    for copy in small:
        copy.start()
    fetch.wait()
    top = jnp.max(loads[...], axis=0)
    n = 12
    for box, here, others in (
        (box_z, z, column),
        (box_b, band, [sibling]),
        (box_x, x, rings[:3]),
        (box_y, y, rings[3:]),
    ):
        box[here] = top
        shared = []
        for other in others:
            shared.append(to_device(box.at[here], box.at[here], sends.at[n], recvs.at[n], other))
            n += 1
        for copy in shared:
            copy.start()
        if box is box_z:
            for copy in large:
                copy.start()
        for copy in shared:
            copy.wait()
        top = jnp.max(box[...], axis=0)
    most[...] = top
    for copy in small + large:
        copy.wait()


def route_tiles(slots, meta, cap, collective_id):
    hbm = pl.BlockSpec(memory_space=pl.ANY)
    return pl.pallas_call(
        functools.partial(route_kernel, cap),
        out_shape=(
            jax.ShapeDtypeStruct((NCLASS, cap, SLOT, TILE), bf16),
            jax.ShapeDtypeStruct((NCLASS, 1, 128), i32),
            jax.ShapeDtypeStruct((1, 128), i32),
        ),
        in_specs=[hbm, hbm],
        out_specs=(hbm, hbm, pl.BlockSpec(memory_space=pltpu.VMEM)),
        scratch_shapes=[
            pltpu.VMEM((NCLASS, 1, 128), i32),
            pltpu.VMEM((4, 1, 128), i32),
            pltpu.VMEM((4, 1, 128), i32),
            pltpu.VMEM((NZ, 1, 128), i32),
            pltpu.VMEM((2, 1, 128), i32),
            pltpu.SemaphoreType.DMA((26,)),
            pltpu.SemaphoreType.DMA((26,)),
            pltpu.SemaphoreType.DMA((3,)),
        ],
        compiler_params=pltpu.CompilerParams(
            collective_id=collective_id, has_side_effects=True, vmem_limit_bytes=4 * MIB
        ),
        name="route",
    )(slots.reshape(NCLASS, 32, SLOT, TILE), meta)


UNROLL = 8


def warp_kernel(cap, meta, recv, slots, out, acc, fac, names, fill):
    _, _, x, y = coords()
    for p in range(32):
        fill[p] = 0

    total = jnp.int32(0)
    for c in range(NCLASS):
        here = meta[c, 0, 3]

        def note(s, carry, c=c, total=total):
            names[total + s] = c * 32 + s
            return carry

        lax.fori_loop(0, here, note, 0)
        total = total + here
    acc[...] = jnp.zeros_like(acc)
    fac[...] = jnp.zeros_like(fac)
    gap = lax.broadcasted_iota(i32, (PATCH, TILE), 0) - lax.broadcasted_iota(i32, (PATCH, TILE), 1)

    def banded(lines, first, gaps, offset):
        gaps = gaps - offset
        mat = jnp.zeros(gaps.shape, f32)
        for b in range(BW):
            mat = jnp.where(gaps == b, lines[first + b : first + b + 1, :], mat)
        return mat.astype(bf16)

    place = lax.broadcasted_iota(i32, (8, TILE), 0)

    def step(i, carry):
        todo = []
        for u in range(UNROLL):
            n = i * UNROLL + u
            at = jnp.minimum(n, total - 1)
            slot = names[at]
            group, rank = slot // 32, slot % 32
            inner = meta[group, 0, rank * 4]
            off_r = meta[group, 0, rank * 4 + 1]
            off_c = meta[group, 0, rank * 4 + 2]
            kept = (group == x) | (group == 4 + y)
            image = jnp.where(kept, slots[slot], recv[group, rank])
            tail = image[TILE:, :].astype(f32)
            live = jnp.where(n < total, 1.0, 0.0).astype(f32)
            colmat = banded(tail, BW, gap, off_c)
            shifted = lax.dot_general(
                image[:TILE, :], colmat, CONTRACT_LAST, preferred_element_type=f32
            ).astype(bf16)
            aligned = pl.multiple_of(jnp.minimum((off_r // 8) * 8, PATCH - WIN), 8)
            rowmat = banded(tail * live, 0, gap[:WIN], off_r - aligned)
            todo.append((n, inner, aligned, tail, jnp.dot(rowmat, shifted, preferred_element_type=f32)))
        for n, inner, aligned, tail, term in todo:
            acc[inner, pl.ds(aligned, WIN), :] += term

            at = fill[inner]
            fill[inner] = at + jnp.where(n < total, 1, 0)
            chosen = jnp.where(n < total, at, FAC)
            for k in range(4):
                rows, lanes = pl.ds(8 * (k // 2), 8), pl.ds(TILE * (k % 2), TILE)
                old = fac[inner, rows, lanes]
                fac[inner, rows, lanes] = jnp.where(place == chosen, tail[8 + k : 9 + k], old)

        return carry

    lax.fori_loop(0, (total + UNROLL - 1) // UNROLL, step, 0)

    def store(p, carry):
        out[p, FAC:, :] = acc[p].astype(bf16)
        out[p, :FAC, :] = fac[p].astype(bf16)
        return carry

    lax.fori_loop(0, 32, store, 0)


def warp_tiles(meta, recv, slots, cap):
    vmem = pl.BlockSpec(memory_space=pltpu.VMEM)
    return pl.pallas_call(
        functools.partial(warp_kernel, cap),
        out_shape=jax.ShapeDtypeStruct((32, PROWS, PATCH), bf16),
        in_specs=[pl.BlockSpec(memory_space=pltpu.SMEM), vmem, vmem],
        out_specs=vmem,
        scratch_shapes=[
            pltpu.VMEM((32, PATCH, PATCH), f32),
            pltpu.VMEM((32, FAC, PATCH), f32),
            pltpu.SMEM((NCLASS * 32,), i32),
            pltpu.SMEM((32,), i32),
        ],
        compiler_params=pltpu.CompilerParams(vmem_limit_bytes=36 * MIB),
        name="warp",
    )(meta, recv, slots)


def merge_kernel(
    part, taps, weight, coadd, detection, recv, zpart, zrecv, mine, other, halo, rowk, colk, sends, recvs
):
    me, z, x, y = coords()
    band = lax.axis_index("band")
    above, below = (me + 127) % 128, (me + 1) % 128
    column = column_partners()
    sibling = {"patch": me, "band": 1 - band}
    near = [{"patch": p, "band": b} for p in (above, below) for b in (band, 1 - band)]
    greet(ring_partners() + column + [sibling] + near)

    def rows_of(c, lead):
        start = 0 if c == 0 else lead + c * CHUNK
        return pl.ds(start, lead + CHUNK if c == 0 else CHUNK)

    def ring_part(c):
        rows = rows_of(c, FAC)
        copies = ring_copies(
            lambda a, i: part.at[1 - a, i, pl.ds(0, 4), rows],
            lambda a, i: recv.at[1 - a, i, pl.ds(0, 4), rows],
            sends,
            recvs,
            6 * c,
        )
        for copy in copies:
            copy.start()
        return copies

    pending = [ring_part(0), ring_part(1)]
    wide = PATCH + 16
    row_gap = lax.broadcasted_iota(i32, (PATCH, wide), 1) - lax.broadcasted_iota(i32, (PATCH, wide), 0) - 4
    col_gap = lax.broadcasted_iota(i32, (PATCH, PATCH), 0) - lax.broadcasted_iota(i32, (PATCH, PATCH), 1) + 4
    row_kernel = jnp.zeros((PATCH, wide), f32)
    col_kernel = jnp.zeros((PATCH, PATCH), f32)
    for r in range(9):
        row_kernel = jnp.where(row_gap == r, taps[r], row_kernel)
        col_kernel = jnp.where(col_gap == r, taps[r], col_kernel)
    rowk[...] = row_kernel
    colk[...] = col_kernel

    zcopies = []
    for c in range(NCHUNK):
        for copy in pending[c]:
            copy.wait()
        if c + 2 < NCHUNK:
            pending.append(ring_part(c + 2))
        for a in range(2):

            own = x if a else y

            def fold(zz, carry, a=a, c=c, own=own):
                if c == 0:
                    zpart[2 * zz + a, :FAC, :] = part[a, own, zz, :FAC, :]
                    for d in range(1, 4):
                        zpart[2 * zz + a, d * FAC : (d + 1) * FAC, :] = recv[a, (own + d) % 4, zz, :FAC, :]
                chunk = pl.ds(FAC + c * CHUNK, CHUNK)
                total = part[a, own, zz, chunk, :].astype(f32)
                for d in range(1, 4):
                    total = total + recv[a, (own + d) % 4, zz, chunk, :].astype(f32)
                at = 4 * FAC + c * CHUNK
                zpart[2 * zz + a, at : at + CHUNK, :] = total.astype(bf16)
                return carry

            lax.fori_loop(0, 4, fold, 0)
        rows = rows_of(c, 4 * FAC)
        copies = []
        for d in (4, 3, 5, 2, 6, 1, 7):
            to = (z + d) % NZ
            n = 6 * NCHUNK + 7 * c + d - 1
            copies.append(
                remote(zpart.at[to, rows], zrecv.at[z, rows], sends.at[n], recvs.at[n], to * 16 + x * 4 + y)
            )
        for copy in copies:
            copy.start()
        zcopies.append(copies)

    cover = None
    last = []
    base = 13 * NCHUNK
    for c in range(NCHUNK):
        for copy in zcopies[c]:
            copy.wait()
        if c == 0:
            row_sums, col_sums = [], []
            for d in range(NZ):
                sums = (zrecv[(z + d) % NZ, : 4 * FAC, :] if d else zpart[z, : 4 * FAC, :]).astype(f32)
                for q in range(4):
                    row_sums.append(sums[q * FAC : q * FAC + 8])
                    col_sums.append(sums[q * FAC + 8 : (q + 1) * FAC])
            cover = lax.dot_general(
                jnp.concatenate(row_sums, axis=0).astype(bf16),
                jnp.concatenate(col_sums, axis=0).astype(bf16),
                CONTRACT_FIRST,
                preferred_element_type=f32,
            )
            mine[...] = jnp.maximum(cover, 1.0)
        chunk = pl.ds(4 * FAC + c * CHUNK, CHUNK)
        total = zpart[z, chunk, :].astype(f32)
        for d in range(1, NZ):
            total = total + zrecv[(z + d) % NZ, chunk, :].astype(f32)
        rows = slice(c * CHUNK, (c + 1) * CHUNK)
        image = total / mine[rows, :]
        coadd[rows, :] = image
        mine[rows, :] = image * weight[0]
        ship = pl.ds(c * CHUNK, CHUNK)
        copies = [to_device(mine.at[ship], other.at[ship], sends.at[base + c], recvs.at[base + c], sibling)]
        if c == 0:
            for n in (0, 1):
                k = base + NCHUNK + n
                copies.append(to_device(mine.at[pl.ds(0, 8)], halo.at[1, n], sends.at[k], recvs.at[k], near[n]))
        if c == NCHUNK - 1:
            for n in (0, 1):
                k = base + NCHUNK + 2 + n
                copies.append(
                    to_device(mine.at[pl.ds(PATCH - 8, 8)], halo.at[0, n], sends.at[k], recvs.at[k], near[2 + n])
                )
        for copy in copies:
            copy.start()
        last += copies
    for copy in last:
        copy.wait()
    top = jnp.where(me == 0, 0.0, halo[0, 0] + halo[0, 1])
    bottom = jnp.where(me == 127, 0.0, halo[1, 0] + halo[1, 1])
    padded = jnp.concatenate([top, mine[...] + other[...], bottom], axis=0)
    row_pass = jnp.dot(rowk[...], padded, precision=lax.Precision.HIGHEST, preferred_element_type=f32)
    detection[...] = jnp.dot(row_pass, colk[...], precision=lax.Precision.HIGHEST, preferred_element_type=f32)


def merge(part, det_taps, band_weight):
    smem = pl.BlockSpec(memory_space=pltpu.SMEM)
    vmem = pl.BlockSpec(memory_space=pltpu.VMEM)
    image = jax.ShapeDtypeStruct((PATCH, PATCH), f32)
    count = 14 * NCHUNK + 4
    return pl.pallas_call(
        merge_kernel,
        out_shape=(image, image),
        in_specs=[vmem, smem, smem],
        out_specs=(vmem, vmem),
        scratch_shapes=[
            pltpu.VMEM((2, 4, 4, PROWS, PATCH), bf16),
            pltpu.VMEM((NZ, ZROWS, PATCH), bf16),
            pltpu.VMEM((NZ, ZROWS, PATCH), bf16),
            pltpu.VMEM((PATCH, PATCH), f32),
            pltpu.VMEM((PATCH, PATCH), f32),
            pltpu.VMEM((2, 2, 8, PATCH), f32),
            pltpu.VMEM((PATCH, PATCH + 16), f32),
            pltpu.VMEM((PATCH, PATCH), f32),
            pltpu.SemaphoreType.DMA((count,)),
            pltpu.SemaphoreType.DMA((count,)),
        ],
        compiler_params=pltpu.CompilerParams(collective_id=2, has_side_effects=True, vmem_limit_bytes=14 * MIB),
        name="merge",
    )(part.reshape(2, 4, 4, PROWS, PATCH), det_taps, band_weight)


def body(
    tiles, psf_coeff, row_taps, col_taps, target_patch, offsets, visits, warp_rows, warp_cols, det_taps, band_weight
):
    info = jnp.concatenate([target_patch[0].T, offsets[0].T, visits], axis=0)

    def widened(lines):
        return jnp.pad(lines, ((0, 16 - lines.shape[0]), (0, BW * TILE - lines.shape[1])))

    packed = [warp_rows[0], warp_cols[0], widened(psf_coeff[0].T), widened(row_taps), widened(col_taps)]
    slots, meta = match_tiles(info, jnp.concatenate(packed, axis=0), tiles[0].reshape(NTILE, TILE, TILE))
    recv, rmeta, most = route_tiles(slots, meta, CAP, 0)

    def few():
        return warp_tiles(rmeta, recv, slots, CAP)

    def many():
        whole, wmeta, _ = route_tiles(slots, meta, 32, 1)
        return warp_tiles(wmeta, whole, slots, 32)

    part = lax.cond(most[0, 3] > CAP, many, few)
    coadd, detection = merge(part, det_taps, band_weight)
    return coadd[None], detection


def solution(mesh):
    in_specs = (
        P("band", "patch", None),
        P("band", "patch", None),
        P(),
        P(),
        P("band", "patch", None),
        P("band", "patch", None),
        P("band", "patch"),
        P("band", "patch", None),
        P("band", "patch", None),
        P(),
        P("band"),
    )
    out_specs = (P("band", "patch", None), P("patch", None))
    return jax.shard_map(body, mesh=mesh, in_specs=in_specs, out_specs=out_specs, check_vma=False)
```

```python
import functools

import jax
import jax.numpy as jnp
from jax import lax
from jax.experimental import pallas as pl
from jax.experimental.pallas import tpu as pltpu
from jax.sharding import PartitionSpec as P

TILE = 128
BW = 4
PATCH = 256
NTILE = 64
NBASIS = 5
TAPS = 41
NCLASS = 8
CAP = 16
SLOT = 144
WIN = 144
FAC = 16
PROWS = PATCH + FAC
ZROWS = PATCH + 4 * FAC
NZ = 8
NCHUNK = 8
CHUNK = PATCH // NCHUNK
MESH = pl.DeviceIdType.MESH
MIB = 1 << 20
STEPS = 4

bf16, f32, i32 = jnp.bfloat16, jnp.float32, jnp.int32
CONTRACT_LAST = (((1,), (1,)), ((), ()))
CONTRACT_FIRST = (((0,), (0,)), ((), ()))


def coords():
    me = lax.axis_index("patch")
    return me, me // 16, (me // 4) % 4, me % 4


def match_kernel(
    info, packed, tiles, slots, meta, images, coef32, coef, gcat, hstack, wr32, wc32, counts, places, loads
):
    chunk = NTILE // STEPS

    def load_of(i):
        part = pl.ds(i * chunk, chunk)
        return pltpu.make_async_copy(tiles.at[part], images.at[part], loads.at[i])

    for i in range(STEPS):
        load_of(i).start()
    coef32[...] = packed[2 * NTILE : 2 * NTILE + 8, :TILE].astype(f32)
    scalars = pltpu.make_async_copy(coef32, coef, loads.at[STEPS])
    scalars.start()
    wr32[...] = packed[:NTILE, :].astype(f32)
    wc32[...] = packed[NTILE : 2 * NTILE, :].astype(f32)
    for n in range(2):
        first = 2 * NTILE + 16 * (n + 1)
        lines = packed[first : first + 16, : 2 * TILE].astype(f32)
        lines = pltpu.roll(lines, 2 * TILE - (TAPS - 1) // 2, 1)
        for k in range(NBASIS):
            full = jnp.broadcast_to(lines[k : k + 1, :], (TILE, 2 * TILE))
            band = pltpu.roll(full, 0, 1, stride=1, stride_axis=0)[:, :TILE].astype(bf16)
            if n == 0:
                gcat[:, k * TILE : (k + 1) * TILE] = band
            else:
                hstack[k * TILE : (k + 1) * TILE, :] = band
    for c in range(NCLASS):
        counts[c] = 0

    for t in range(NTILE):
        target = info[0, t]
        pz, px, py = target // 16, (target // 4) % 4, target % 4
        even = (pz % 2) == 0
        group = jnp.where(even, px, 4 + py)
        rank = counts[group]
        counts[group] = rank + 1
        places[t] = group * 32 + rank
        meta[group, 0, rank * 4] = jnp.where(even, py, px) * 4 + pz // 2 + jnp.where(even, 0, 16)
        meta[group, 0, rank * 4 + 1] = info[1, t]
        meta[group, 0, rank * 4 + 2] = info[2, t]
    for c in range(NCLASS):
        meta[c, 0, 3] = counts[c]
    def placed(line, offset):
        wide = jnp.concatenate([line, jnp.zeros((BW, TILE), f32)], axis=1)
        wide = jnp.concatenate([wide, jnp.zeros((8 - BW, 2 * TILE), f32)], axis=0)
        summed = jnp.sum(pltpu.roll(wide, 0, 1, stride=1, stride_axis=0), axis=0, keepdims=True)
        return pltpu.roll(summed, offset, 1)

    def tapped(line):
        return jnp.concatenate([line[:, b * TILE : (b + 1) * TILE] for b in range(BW)], axis=0)

    def pack(t):
        off_r, off_c, visit = info[1, t], info[2, t], info[3, t]
        row_line = tapped((wr32[pl.ds(t, 1), :] * visit.astype(f32)).astype(bf16).astype(f32))
        col_line = tapped(wc32[pl.ds(t, 1), :])
        row_sum = placed(row_line, off_r)
        col_sum = placed(col_line, off_c)
        tail = [row_line, col_line]
        tail += [row_sum[:, :TILE], row_sum[:, TILE:], col_sum[:, :TILE], col_sum[:, TILE:]]
        tail += [jnp.zeros((4, TILE), f32)]
        return jnp.concatenate(tail, axis=0).astype(bf16)

    def step(i, carry):
        load_of(i).wait()
        for v in range(chunk // 2):
            first = i * chunk + 2 * v
            pair = images[pl.ds(first, 2)].reshape(2 * TILE, TILE)
            part = lax.dot_general(pair, hstack[...], CONTRACT_LAST, preferred_element_type=f32)
            columns = []
            for u in range(2):
                rows = part[u * TILE : (u + 1) * TILE]
                blocks = [
                    (rows[:, k * TILE : (k + 1) * TILE] * coef[k, first + u]).astype(bf16)
                    for k in range(NBASIS)
                ]
                columns.append(jnp.concatenate(blocks, axis=0))
            scaled = jnp.concatenate(columns, axis=1)
            matched = jnp.dot(gcat[...], scaled, preferred_element_type=f32).astype(bf16)
            for u in range(2):
                at = places[first + u]
                slots[at, :TILE, :] = matched[:, u * TILE : (u + 1) * TILE]
                slots[at, TILE:, :] = pack(first + u)
        return carry

    scalars.wait()
    lax.fori_loop(0, STEPS, step, 0)


def match_tiles(info, packed, tiles):
    smem = pl.BlockSpec(memory_space=pltpu.SMEM)
    vmem = pl.BlockSpec(memory_space=pltpu.VMEM)
    return pl.pallas_call(
        match_kernel,
        out_shape=(
            jax.ShapeDtypeStruct((NCLASS * 32, SLOT, TILE), bf16),
            jax.ShapeDtypeStruct((NCLASS, 1, 128), i32),
        ),
        in_specs=[smem, vmem, pl.BlockSpec(memory_space=pl.ANY)],
        out_specs=(vmem, smem),
        scratch_shapes=[
            pltpu.VMEM((NTILE, TILE, TILE), bf16),
            pltpu.VMEM((8, 128), f32),
            pltpu.SMEM((8, 128), f32),
            pltpu.VMEM((TILE, NBASIS * TILE), bf16),
            pltpu.VMEM((NBASIS * TILE, TILE), bf16),
            pltpu.VMEM((NTILE, BW * TILE), f32),
            pltpu.VMEM((NTILE, BW * TILE), f32),
            pltpu.SMEM((NCLASS,), i32),
            pltpu.SMEM((NTILE,), i32),
            pltpu.SemaphoreType.DMA((STEPS + 1,)),
        ],
        compiler_params=pltpu.CompilerParams(vmem_limit_bytes=24 * MIB),
        name="match",
    )(info, packed, tiles)


def greet(partners):
    barrier = pltpu.get_barrier_semaphore()
    for partner in partners:
        pl.semaphore_signal(barrier, inc=1, device_id=partner, device_id_type=MESH)
    pl.semaphore_wait(barrier, len(partners))


def remote(src, dst, send, recv, patch):
    return pltpu.make_async_remote_copy(
        src_ref=src, dst_ref=dst, send_sem=send, recv_sem=recv, device_id={"patch": patch}, device_id_type=MESH
    )


def ring_copies(send_block, recv_block, sends, recvs, first):
    me, z, x, y = coords()
    copies = []
    for d in (2, 1, 3):
        for axis, here in ((0, x), (1, y)):
            there = (here + d) % 4
            owner = z * 16 + there * 4 + y if axis == 0 else z * 16 + x * 4 + there
            n = first + len(copies)
            copies.append(remote(send_block(axis, there), recv_block(axis, here), sends.at[n], recvs.at[n], owner))
    return copies


def ring_partners():
    me, z, x, y = coords()
    partners = [{"patch": z * 16 + ((x + d) % 4) * 4 + y} for d in (1, 2, 3)]
    return partners + [{"patch": z * 16 + x * 4 + (y + d) % 4} for d in (1, 2, 3)]


def column_partners():
    me, z, x, y = coords()
    return [{"patch": ((z + d) % NZ) * 16 + x * 4 + y} for d in range(1, NZ)]


def to_device(src, dst, send, recv, device):
    return pltpu.make_async_remote_copy(
        src_ref=src, dst_ref=dst, send_sem=send, recv_sem=recv, device_id=device, device_id_type=MESH
    )


def route_kernel(cap, slots, meta, recv, rmeta, most, box_p, box_z, box_b, sends, recvs, local):
    me, z, x, y = coords()
    band = lax.axis_index("band")
    column = column_partners()
    plane = [{"patch": z * 16 + lax.rem(me % 16 + d, 16)} for d in range(1, 16)]
    sibling = {"patch": me, "band": 1 - band}
    greet(plane + column + [sibling])
    small = ring_copies(lambda a, i: meta.at[4 * a + i], lambda a, i: rmeta.at[4 * a + i], sends, recvs, 6)
    for n, own in enumerate((x, 4 + y)):
        small.append(pltpu.make_async_copy(meta.at[own], rmeta.at[own], local.at[n]))
    large = ring_copies(
        lambda a, i: slots.at[4 * a + i, pl.ds(0, cap)], lambda a, i: recv.at[4 * a + i], sends, recvs, 0
    )
    top = jnp.max(meta[...], axis=0)
    n = 12
    for box, here, others in (
        (box_p, me % 16, plane),
        (box_z, z, column),
        (box_b, band, [sibling]),
    ):
        box[here] = top
        shared = []
        for other in others:
            shared.append(to_device(box.at[here], box.at[here], sends.at[n], recvs.at[n], other))
            n += 1
        for copy in shared:
            copy.start()
        if box is box_p:
            for copy in small + large:
                copy.start()
        for copy in shared:
            copy.wait()
        top = jnp.max(box[...], axis=0)
    most[...] = top
    for copy in small + large:
        copy.wait()


def route_tiles(slots, meta, cap, collective_id):
    hbm = pl.BlockSpec(memory_space=pl.ANY)
    return pl.pallas_call(
        functools.partial(route_kernel, cap),
        out_shape=(
            jax.ShapeDtypeStruct((NCLASS, cap, SLOT, TILE), bf16),
            jax.ShapeDtypeStruct((NCLASS, 1, 128), i32),
            jax.ShapeDtypeStruct((1, 128), i32),
        ),
        in_specs=[hbm, pl.BlockSpec(memory_space=pltpu.VMEM)],
        out_specs=(hbm, hbm, pl.BlockSpec(memory_space=pltpu.VMEM)),
        scratch_shapes=[
            pltpu.VMEM((16, 1, 128), i32),
            pltpu.VMEM((NZ, 1, 128), i32),
            pltpu.VMEM((2, 1, 128), i32),
            pltpu.SemaphoreType.DMA((35,)),
            pltpu.SemaphoreType.DMA((35,)),
            pltpu.SemaphoreType.DMA((2,)),
        ],
        compiler_params=pltpu.CompilerParams(
            collective_id=collective_id, has_side_effects=True, vmem_limit_bytes=4 * MIB
        ),
        name="route",
    )(slots.reshape(NCLASS, 32, SLOT, TILE), meta)


UNROLL = 8


def warp_kernel(cap, meta, recv, slots, out, acc, fac, names, fill):
    _, _, x, y = coords()
    for p in range(32):
        fill[p] = 0

    total = jnp.int32(0)
    for c in range(NCLASS):
        here = meta[c, 0, 3]

        def note(s, carry, c=c, total=total):
            names[total + s] = c * 32 + s
            return carry

        lax.fori_loop(0, here, note, 0)
        total = total + here
    acc[...] = jnp.zeros_like(acc)
    fac[...] = jnp.zeros_like(fac)
    gap = lax.broadcasted_iota(i32, (PATCH, TILE), 0) - lax.broadcasted_iota(i32, (PATCH, TILE), 1)
    gap = gap.astype(jnp.int16)

    def banded(lines, first, gaps, offset):
        gaps = gaps - offset.astype(jnp.int16)
        mat = jnp.zeros(gaps.shape, bf16)
        for b in range(BW):
            line = lines[first + b : first + b + 1, :].astype(bf16)
            mat = jnp.where(gaps == jnp.int16(b), line, mat)
        return mat

    place = lax.broadcasted_iota(i32, (8, TILE), 0)

    def step(i, carry):
        todo = []
        for u in range(UNROLL):
            n = i * UNROLL + u
            at = jnp.minimum(n, total - 1)
            slot = names[at]
            group, rank = slot // 32, slot % 32
            inner = meta[group, 0, rank * 4]
            off_r = meta[group, 0, rank * 4 + 1]
            off_c = meta[group, 0, rank * 4 + 2]
            kept = (group == x) | (group == 4 + y)
            image = jnp.where(kept, slots[slot], recv[group, rank])
            tail = image[TILE:, :].astype(f32)
            live = jnp.where(n < total, 1.0, 0.0).astype(f32)
            colmat = banded(tail, BW, gap, off_c)
            shifted = lax.dot_general(
                image[:TILE, :], colmat, CONTRACT_LAST, preferred_element_type=f32
            ).astype(bf16)
            aligned = pl.multiple_of(jnp.minimum((off_r // 8) * 8, PATCH - WIN), 8)
            rowmat = banded(tail * live, 0, gap[:WIN], off_r - aligned)
            todo.append((n, inner, aligned, tail, jnp.dot(rowmat, shifted, preferred_element_type=f32)))
        for n, inner, aligned, tail, term in todo:
            acc[inner, pl.ds(aligned, WIN), :] += term

            at = fill[inner]
            fill[inner] = at + jnp.where(n < total, 1, 0)
            chosen = jnp.where(n < total, at, FAC)
            for k in range(4):
                rows, lanes = pl.ds(8 * (k // 2), 8), pl.ds(TILE * (k % 2), TILE)
                old = fac[inner, rows, lanes]
                fac[inner, rows, lanes] = jnp.where(place == chosen, tail[8 + k : 9 + k], old)

        return carry

    lax.fori_loop(0, (total + UNROLL - 1) // UNROLL, step, 0)

    def store(p, carry):
        out[p, FAC:, :] = acc[p].astype(bf16)
        out[p, :FAC, :] = fac[p].astype(bf16)
        return carry

    lax.fori_loop(0, 32, store, 0)


def warp_tiles(meta, recv, slots, cap):
    vmem = pl.BlockSpec(memory_space=pltpu.VMEM)
    return pl.pallas_call(
        functools.partial(warp_kernel, cap),
        out_shape=jax.ShapeDtypeStruct((32, PROWS, PATCH), bf16),
        in_specs=[pl.BlockSpec(memory_space=pltpu.SMEM), vmem, vmem],
        out_specs=vmem,
        scratch_shapes=[
            pltpu.VMEM((32, PATCH, PATCH), f32),
            pltpu.VMEM((32, FAC, PATCH), f32),
            pltpu.SMEM((NCLASS * 32,), i32),
            pltpu.SMEM((32,), i32),
        ],
        compiler_params=pltpu.CompilerParams(vmem_limit_bytes=36 * MIB),
        name="warp",
    )(meta, recv, slots)


def dot3(a, b):
    a_high, b_high = a.astype(bf16), b.astype(bf16)
    a_low, b_low = (a - a_high.astype(f32)).astype(bf16), (b - b_high.astype(f32)).astype(bf16)

    def dot(p, q):
        return jnp.dot(p, q, preferred_element_type=f32)

    return dot(a_high, b_high) + (dot(a_low, b_high) + dot(a_high, b_low))


def merge_kernel(
    part, taps, weight, coadd, detection, recv, zpart, zrecv, mine, other, halo, rowk, colk, sends, recvs
):
    me, z, x, y = coords()
    band = lax.axis_index("band")
    above, below = (me + 127) % 128, (me + 1) % 128
    column = column_partners()
    sibling = {"patch": me, "band": 1 - band}
    near = [{"patch": p, "band": b} for p in (above, below) for b in (band, 1 - band)]
    greet(ring_partners() + column + [sibling] + near)

    def rows_of(c, lead):
        start = 0 if c == 0 else lead + c * CHUNK
        return pl.ds(start, lead + CHUNK if c == 0 else CHUNK)

    def ring_part(c):
        rows = rows_of(c, FAC)
        copies = ring_copies(
            lambda a, i: part.at[1 - a, i, pl.ds(0, 4), rows],
            lambda a, i: recv.at[1 - a, i, pl.ds(0, 4), rows],
            sends,
            recvs,
            6 * c,
        )
        for copy in copies:
            copy.start()
        return copies

    pending = [ring_part(0), ring_part(1)]
    wide = PATCH + 16
    row_gap = lax.broadcasted_iota(i32, (PATCH, wide), 1) - lax.broadcasted_iota(i32, (PATCH, wide), 0) - 4
    col_gap = lax.broadcasted_iota(i32, (PATCH, PATCH), 0) - lax.broadcasted_iota(i32, (PATCH, PATCH), 1) + 4
    row_kernel = jnp.zeros((PATCH, wide), f32)
    col_kernel = jnp.zeros((PATCH, PATCH), f32)
    for r in range(9):
        row_kernel = jnp.where(row_gap == r, taps[r], row_kernel)
        col_kernel = jnp.where(col_gap == r, taps[r], col_kernel)
    rowk[...] = row_kernel
    colk[...] = col_kernel

    zcopies = []
    for c in range(NCHUNK):
        for copy in pending[c]:
            copy.wait()
        if c + 2 < NCHUNK:
            pending.append(ring_part(c + 2))
        for a in range(2):

            own = x if a else y

            def fold(zz, carry, a=a, c=c, own=own):
                if c == 0:
                    zpart[2 * zz + a, :FAC, :] = part[a, own, zz, :FAC, :]
                    for d in range(1, 4):
                        zpart[2 * zz + a, d * FAC : (d + 1) * FAC, :] = recv[a, (own + d) % 4, zz, :FAC, :]
                chunk = pl.ds(FAC + c * CHUNK, CHUNK)
                total = part[a, own, zz, chunk, :].astype(f32)
                for d in range(1, 4):
                    total = total + recv[a, (own + d) % 4, zz, chunk, :].astype(f32)
                at = 4 * FAC + c * CHUNK
                zpart[2 * zz + a, at : at + CHUNK, :] = total.astype(bf16)
                return carry

            lax.fori_loop(0, 4, fold, 0)
        rows = rows_of(c, 4 * FAC)
        copies = []
        for d in (4, 3, 5, 2, 6, 1, 7):
            to = (z + d) % NZ
            n = 6 * NCHUNK + 7 * c + d - 1
            copies.append(
                remote(zpart.at[to, rows], zrecv.at[z, rows], sends.at[n], recvs.at[n], to * 16 + x * 4 + y)
            )
        for copy in copies:
            copy.start()
        zcopies.append(copies)

    cover = None
    last = []
    base = 13 * NCHUNK
    for c in range(NCHUNK):
        for copy in zcopies[c]:
            copy.wait()
        if c == 0:
            row_sums, col_sums = [], []
            for d in range(NZ):
                sums = (zrecv[(z + d) % NZ, : 4 * FAC, :] if d else zpart[z, : 4 * FAC, :]).astype(f32)
                for q in range(4):
                    row_sums.append(sums[q * FAC : q * FAC + 8])
                    col_sums.append(sums[q * FAC + 8 : (q + 1) * FAC])
            cover = lax.dot_general(
                jnp.concatenate(row_sums, axis=0).astype(bf16),
                jnp.concatenate(col_sums, axis=0).astype(bf16),
                CONTRACT_FIRST,
                preferred_element_type=f32,
            )
            mine[...] = jnp.maximum(cover, 1.0)
        chunk = pl.ds(4 * FAC + c * CHUNK, CHUNK)
        total = zpart[z, chunk, :].astype(f32)
        for d in range(1, NZ):
            total = total + zrecv[(z + d) % NZ, chunk, :].astype(f32)
        rows = slice(c * CHUNK, (c + 1) * CHUNK)
        image = total / mine[rows, :]
        coadd[rows, :] = image
        mine[rows, :] = image * weight[0]
        ship = pl.ds(c * CHUNK, CHUNK)
        copies = [to_device(mine.at[ship], other.at[ship], sends.at[base + c], recvs.at[base + c], sibling)]
        if c == 0:
            for n in (0, 1):
                k = base + NCHUNK + n
                copies.append(to_device(mine.at[pl.ds(0, 8)], halo.at[1, n], sends.at[k], recvs.at[k], near[n]))
        if c == NCHUNK - 1:
            for n in (0, 1):
                k = base + NCHUNK + 2 + n
                copies.append(
                    to_device(mine.at[pl.ds(PATCH - 8, 8)], halo.at[0, n], sends.at[k], recvs.at[k], near[2 + n])
                )
        for copy in copies:
            copy.start()
        last += copies
    for copy in last:
        copy.wait()
    top = jnp.where(me == 0, 0.0, halo[0, 0] + halo[0, 1])
    bottom = jnp.where(me == 127, 0.0, halo[1, 0] + halo[1, 1])
    padded = jnp.concatenate([top, mine[...] + other[...], bottom], axis=0)
    row_pass = dot3(rowk[...], padded)
    detection[...] = dot3(row_pass, colk[...])


def merge(part, det_taps, band_weight):
    smem = pl.BlockSpec(memory_space=pltpu.SMEM)
    vmem = pl.BlockSpec(memory_space=pltpu.VMEM)
    image = jax.ShapeDtypeStruct((PATCH, PATCH), f32)
    count = 14 * NCHUNK + 4
    return pl.pallas_call(
        merge_kernel,
        out_shape=(image, image),
        in_specs=[vmem, smem, smem],
        out_specs=(vmem, vmem),
        scratch_shapes=[
            pltpu.VMEM((2, 4, 4, PROWS, PATCH), bf16),
            pltpu.VMEM((NZ, ZROWS, PATCH), bf16),
            pltpu.VMEM((NZ, ZROWS, PATCH), bf16),
            pltpu.VMEM((PATCH, PATCH), f32),
            pltpu.VMEM((PATCH, PATCH), f32),
            pltpu.VMEM((2, 2, 8, PATCH), f32),
            pltpu.VMEM((PATCH, PATCH + 16), f32),
            pltpu.VMEM((PATCH, PATCH), f32),
            pltpu.SemaphoreType.DMA((count,)),
            pltpu.SemaphoreType.DMA((count,)),
        ],
        compiler_params=pltpu.CompilerParams(collective_id=2, has_side_effects=True, vmem_limit_bytes=14 * MIB),
        name="merge",
    )(part.reshape(2, 4, 4, PROWS, PATCH), det_taps, band_weight)


def body(
    tiles, psf_coeff, row_taps, col_taps, target_patch, offsets, visits, warp_rows, warp_cols, det_taps, band_weight
):
    info = jnp.concatenate([target_patch[0].T, offsets[0].T, visits], axis=0)

    def widened(lines):
        return jnp.pad(lines, ((0, 16 - lines.shape[0]), (0, BW * TILE - lines.shape[1])))

    packed = [warp_rows[0], warp_cols[0], widened(psf_coeff[0].T), widened(row_taps), widened(col_taps)]
    slots, meta = match_tiles(info, jnp.concatenate(packed, axis=0), tiles[0].reshape(NTILE, TILE, TILE))
    recv, rmeta, most = route_tiles(slots, meta, CAP, 0)

    def few():
        return warp_tiles(rmeta, recv, slots, CAP)

    def many():
        whole, wmeta, _ = route_tiles(slots, meta, 32, 1)
        return warp_tiles(wmeta, whole, slots, 32)

    part = lax.cond(most[0, 3] > CAP, many, few)
    coadd, detection = merge(part, det_taps, band_weight)
    return coadd[None], detection


def solution(mesh):
    in_specs = (
        P("band", "patch", None),
        P("band", "patch", None),
        P(),
        P(),
        P("band", "patch", None),
        P("band", "patch", None),
        P("band", "patch"),
        P("band", "patch", None),
        P("band", "patch", None),
        P(),
        P("band"),
    )
    out_specs = (P("band", "patch", None), P("patch", None))
    return jax.shard_map(body, mesh=mesh, in_specs=in_specs, out_specs=out_specs, check_vma=False)
```

```python
import functools

import jax
import jax.numpy as jnp
from jax import lax
from jax.experimental import pallas as pl
from jax.experimental.pallas import tpu as pltpu
from jax.sharding import PartitionSpec as P

TILE = 128
BW = 4
PATCH = 256
NTILE = 64
NBASIS = 5
TAPS = 41
NCLASS = 8
CAP = 16
SLOT = 144
WIN = 144
FAC = 16
PROWS = PATCH + FAC
ZROWS = PATCH + 4 * FAC
NZ = 8
NCHUNK = 8
CHUNK = PATCH // NCHUNK
MESH = pl.DeviceIdType.MESH
MIB = 1 << 20
STEPS = 4

bf16, f32, i32 = jnp.bfloat16, jnp.float32, jnp.int32
CONTRACT_LAST = (((1,), (1,)), ((), ()))
CONTRACT_FIRST = (((0,), (0,)), ((), ()))


def coords():
    me = lax.axis_index("patch")
    return me, me // 16, (me // 4) % 4, me % 4


def match_kernel(
    info, packed, tiles, slots, meta, images, coef32, coef, gcat, hstack, wr32, wc32, counts, places, loads
):
    chunk = NTILE // STEPS

    def load_of(i):
        part = pl.ds(i * chunk, chunk)
        return pltpu.make_async_copy(tiles.at[part], images.at[part], loads.at[i])

    for i in range(STEPS):
        load_of(i).start()
    coef32[...] = packed[2 * NTILE : 2 * NTILE + 8, :TILE].astype(f32)
    scalars = pltpu.make_async_copy(coef32, coef, loads.at[STEPS])
    scalars.start()
    wr32[...] = packed[:NTILE, :].astype(f32)
    wc32[...] = packed[NTILE : 2 * NTILE, :].astype(f32)
    for n in range(2):
        first = 2 * NTILE + 16 * (n + 1)
        lines = packed[first : first + 16, : 2 * TILE].astype(f32)
        lines = pltpu.roll(lines, 2 * TILE - (TAPS - 1) // 2, 1)
        for k in range(NBASIS):
            full = jnp.broadcast_to(lines[k : k + 1, :], (TILE, 2 * TILE))
            band = pltpu.roll(full, 0, 1, stride=1, stride_axis=0)[:, :TILE].astype(bf16)
            if n == 0:
                gcat[:, k * TILE : (k + 1) * TILE] = band
            else:
                hstack[k * TILE : (k + 1) * TILE, :] = band
    for c in range(NCLASS):
        counts[c] = 0

    for t in range(NTILE):
        target = info[0, t]
        pz, px, py = target // 16, (target // 4) % 4, target % 4
        even = (pz % 2) == 0
        group = jnp.where(even, px, 4 + py)
        rank = counts[group]
        counts[group] = rank + 1
        places[t] = group * 32 + rank
        meta[group, 0, rank * 4] = jnp.where(even, py, px) * 4 + pz // 2 + jnp.where(even, 0, 16)
        meta[group, 0, rank * 4 + 1] = info[1, t]
        meta[group, 0, rank * 4 + 2] = info[2, t]
    for c in range(NCLASS):
        meta[c, 0, 3] = counts[c]
    def placed(line, offset):
        wide = jnp.concatenate([line, jnp.zeros((BW, TILE), f32)], axis=1)
        wide = jnp.concatenate([wide, jnp.zeros((8 - BW, 2 * TILE), f32)], axis=0)
        summed = jnp.sum(pltpu.roll(wide, 0, 1, stride=1, stride_axis=0), axis=0, keepdims=True)
        return pltpu.roll(summed, offset, 1)

    def tapped(line):
        return jnp.concatenate([line[:, b * TILE : (b + 1) * TILE] for b in range(BW)], axis=0)

    def pack(t):
        off_r, off_c, visit = info[1, t], info[2, t], info[3, t]
        row_line = tapped((wr32[pl.ds(t, 1), :] * visit.astype(f32)).astype(bf16).astype(f32))
        col_line = tapped(wc32[pl.ds(t, 1), :])
        row_sum = placed(row_line, off_r)
        col_sum = placed(col_line, off_c)
        tail = [row_line, col_line]
        tail += [row_sum[:, :TILE], row_sum[:, TILE:], col_sum[:, :TILE], col_sum[:, TILE:]]
        tail += [jnp.zeros((4, TILE), f32)]
        return jnp.concatenate(tail, axis=0).astype(bf16)

    def step(i, carry):
        load_of(i).wait()
        for v in range(chunk // 2):
            first = i * chunk + 2 * v
            pair = images[pl.ds(first, 2)].reshape(2 * TILE, TILE)
            part = lax.dot_general(pair, hstack[...], CONTRACT_LAST, preferred_element_type=f32)
            columns = []
            for u in range(2):
                rows = part[u * TILE : (u + 1) * TILE]
                blocks = [
                    (rows[:, k * TILE : (k + 1) * TILE] * coef[k, first + u]).astype(bf16)
                    for k in range(NBASIS)
                ]
                columns.append(jnp.concatenate(blocks, axis=0))
            scaled = jnp.concatenate(columns, axis=1)
            matched = jnp.dot(gcat[...], scaled, preferred_element_type=f32).astype(bf16)
            for u in range(2):
                at = places[first + u]
                slots[at, :TILE, :] = matched[:, u * TILE : (u + 1) * TILE]
                slots[at, TILE:, :] = pack(first + u)
        return carry

    scalars.wait()
    lax.fori_loop(0, STEPS, step, 0)


def match_tiles(info, packed, tiles):
    smem = pl.BlockSpec(memory_space=pltpu.SMEM)
    vmem = pl.BlockSpec(memory_space=pltpu.VMEM)
    return pl.pallas_call(
        match_kernel,
        out_shape=(
            jax.ShapeDtypeStruct((NCLASS * 32, SLOT, TILE), bf16),
            jax.ShapeDtypeStruct((NCLASS, 1, 128), i32),
        ),
        in_specs=[smem, vmem, pl.BlockSpec(memory_space=pl.ANY)],
        out_specs=(vmem, smem),
        scratch_shapes=[
            pltpu.VMEM((NTILE, TILE, TILE), bf16),
            pltpu.VMEM((8, 128), f32),
            pltpu.SMEM((8, 128), f32),
            pltpu.VMEM((TILE, NBASIS * TILE), bf16),
            pltpu.VMEM((NBASIS * TILE, TILE), bf16),
            pltpu.VMEM((NTILE, BW * TILE), f32),
            pltpu.VMEM((NTILE, BW * TILE), f32),
            pltpu.SMEM((NCLASS,), i32),
            pltpu.SMEM((NTILE,), i32),
            pltpu.SemaphoreType.DMA((STEPS + 1,)),
        ],
        compiler_params=pltpu.CompilerParams(vmem_limit_bytes=24 * MIB),
        name="match",
    )(info, packed, tiles)


def greet(partners):
    barrier = pltpu.get_barrier_semaphore()
    for partner in partners:
        pl.semaphore_signal(barrier, inc=1, device_id=partner, device_id_type=MESH)
    pl.semaphore_wait(barrier, len(partners))


def remote(src, dst, send, recv, patch):
    return pltpu.make_async_remote_copy(
        src_ref=src, dst_ref=dst, send_sem=send, recv_sem=recv, device_id={"patch": patch}, device_id_type=MESH
    )


def ring_copies(send_block, recv_block, sends, recvs, first):
    me, z, x, y = coords()
    copies = []
    for d in (1, 3, 2):
        for axis, here in ((0, x), (1, y)):
            there = (here + d) % 4
            owner = z * 16 + there * 4 + y if axis == 0 else z * 16 + x * 4 + there
            n = first + len(copies)
            copies.append(remote(send_block(axis, there), recv_block(axis, here), sends.at[n], recvs.at[n], owner))
    return copies


def ring_partners():
    me, z, x, y = coords()
    partners = [{"patch": z * 16 + ((x + d) % 4) * 4 + y} for d in (1, 2, 3)]
    return partners + [{"patch": z * 16 + x * 4 + (y + d) % 4} for d in (1, 2, 3)]


def column_partners():
    me, z, x, y = coords()
    return [{"patch": ((z + d) % NZ) * 16 + x * 4 + y} for d in range(1, NZ)]


def to_device(src, dst, send, recv, device):
    return pltpu.make_async_remote_copy(
        src_ref=src, dst_ref=dst, send_sem=send, recv_sem=recv, device_id=device, device_id_type=MESH
    )


def route_kernel(cap, slots, meta, recv, rmeta, most, box_p, box_z, box_b, sends, recvs, local):
    me, z, x, y = coords()
    band = lax.axis_index("band")
    column = column_partners()
    plane = [{"patch": z * 16 + lax.rem(me % 16 + d, 16)} for d in range(1, 16)]
    sibling = {"patch": me, "band": 1 - band}
    greet(plane + column + [sibling])
    small = ring_copies(lambda a, i: meta.at[4 * a + i], lambda a, i: rmeta.at[4 * a + i], sends, recvs, 6)
    for n, own in enumerate((x, 4 + y)):
        small.append(pltpu.make_async_copy(meta.at[own], rmeta.at[own], local.at[n]))
    large = ring_copies(
        lambda a, i: slots.at[4 * a + i, pl.ds(0, cap)], lambda a, i: recv.at[4 * a + i], sends, recvs, 0
    )
    top = jnp.max(meta[...], axis=0)
    n = 12
    for box, here, others in (
        (box_p, me % 16, plane),
        (box_z, z, column),
        (box_b, band, [sibling]),
    ):
        box[here] = top
        shared = []
        for other in others:
            shared.append(to_device(box.at[here], box.at[here], sends.at[n], recvs.at[n], other))
            n += 1
        for copy in shared:
            copy.start()
        if box is box_p:
            for copy in small + large:
                copy.start()
        for copy in shared:
            copy.wait()
        top = jnp.max(box[...], axis=0)
    most[...] = top
    for copy in small + large:
        copy.wait()


def route_tiles(slots, meta, cap, collective_id):
    hbm = pl.BlockSpec(memory_space=pl.ANY)
    return pl.pallas_call(
        functools.partial(route_kernel, cap),
        out_shape=(
            jax.ShapeDtypeStruct((NCLASS, cap, SLOT, TILE), bf16),
            jax.ShapeDtypeStruct((NCLASS, 1, 128), i32),
            jax.ShapeDtypeStruct((1, 128), i32),
        ),
        in_specs=[hbm, pl.BlockSpec(memory_space=pltpu.VMEM)],
        out_specs=(hbm, hbm, pl.BlockSpec(memory_space=pltpu.VMEM)),
        scratch_shapes=[
            pltpu.VMEM((16, 1, 128), i32),
            pltpu.VMEM((NZ, 1, 128), i32),
            pltpu.VMEM((2, 1, 128), i32),
            pltpu.SemaphoreType.DMA((35,)),
            pltpu.SemaphoreType.DMA((35,)),
            pltpu.SemaphoreType.DMA((2,)),
        ],
        compiler_params=pltpu.CompilerParams(
            collective_id=collective_id, has_side_effects=True, vmem_limit_bytes=4 * MIB
        ),
        name="route",
    )(slots.reshape(NCLASS, 32, SLOT, TILE), meta)


UNROLL = 8


def warp_kernel(cap, meta, recv, slots, out, acc, fac, names, fill):
    _, _, x, y = coords()
    for p in range(32):
        fill[p] = 0

    total = jnp.int32(0)
    for c in range(NCLASS):
        here = meta[c, 0, 3]

        def note(s, carry, c=c, total=total):
            names[total + s] = c * 32 + s
            return carry

        lax.fori_loop(0, here, note, 0)
        total = total + here
    acc[...] = jnp.zeros_like(acc)
    fac[...] = jnp.zeros_like(fac)
    gap = lax.broadcasted_iota(i32, (PATCH, TILE), 0) - lax.broadcasted_iota(i32, (PATCH, TILE), 1)
    gap = gap.astype(jnp.int16)

    def banded(lines, first, gaps, offset):
        gaps = gaps - offset.astype(jnp.int16)
        mat = jnp.zeros(gaps.shape, bf16)
        for b in range(BW):
            line = lines[first + b : first + b + 1, :].astype(bf16)
            mat = jnp.where(gaps == jnp.int16(b), line, mat)
        return mat

    place = lax.broadcasted_iota(i32, (8, TILE), 0)

    def step(i, carry):
        todo = []
        for u in range(UNROLL):
            n = i * UNROLL + u
            at = jnp.minimum(n, total - 1)
            slot = names[at]
            group, rank = slot // 32, slot % 32
            inner = meta[group, 0, rank * 4]
            off_r = meta[group, 0, rank * 4 + 1]
            off_c = meta[group, 0, rank * 4 + 2]
            kept = (group == x) | (group == 4 + y)
            image = jnp.where(kept, slots[slot], recv[group, rank])
            tail = image[TILE:, :].astype(f32)
            live = jnp.where(n < total, 1.0, 0.0).astype(f32)
            colmat = banded(tail, BW, gap, off_c)
            shifted = lax.dot_general(
                image[:TILE, :], colmat, CONTRACT_LAST, preferred_element_type=f32
            ).astype(bf16)
            aligned = pl.multiple_of(jnp.minimum((off_r // 8) * 8, PATCH - WIN), 8)
            rowmat = banded(tail * live, 0, gap[:WIN], off_r - aligned)
            todo.append((n, inner, aligned, tail, jnp.dot(rowmat, shifted, preferred_element_type=f32)))
        for n, inner, aligned, tail, term in todo:
            acc[inner, pl.ds(aligned, WIN), :] += term

            at = fill[inner]
            fill[inner] = at + jnp.where(n < total, 1, 0)
            chosen = jnp.where(n < total, at, FAC)
            for k in range(4):
                rows, lanes = pl.ds(8 * (k // 2), 8), pl.ds(TILE * (k % 2), TILE)
                old = fac[inner, rows, lanes]
                fac[inner, rows, lanes] = jnp.where(place == chosen, tail[8 + k : 9 + k], old)

        return carry

    lax.fori_loop(0, (total + UNROLL - 1) // UNROLL, step, 0)

    def store(p, carry):
        out[p, FAC:, :] = acc[p].astype(bf16)
        out[p, :FAC, :] = fac[p].astype(bf16)
        return carry

    lax.fori_loop(0, 32, store, 0)


def warp_tiles(meta, recv, slots, cap):
    vmem = pl.BlockSpec(memory_space=pltpu.VMEM)
    return pl.pallas_call(
        functools.partial(warp_kernel, cap),
        out_shape=jax.ShapeDtypeStruct((32, PROWS, PATCH), bf16),
        in_specs=[pl.BlockSpec(memory_space=pltpu.SMEM), vmem, vmem],
        out_specs=vmem,
        scratch_shapes=[
            pltpu.VMEM((32, PATCH, PATCH), f32),
            pltpu.VMEM((32, FAC, PATCH), f32),
            pltpu.SMEM((NCLASS * 32,), i32),
            pltpu.SMEM((32,), i32),
        ],
        compiler_params=pltpu.CompilerParams(vmem_limit_bytes=36 * MIB),
        name="warp",
    )(meta, recv, slots)


def dot3(a, b):
    a_high, b_high = a.astype(bf16), b.astype(bf16)
    a_low, b_low = (a - a_high.astype(f32)).astype(bf16), (b - b_high.astype(f32)).astype(bf16)

    def dot(p, q):
        return jnp.dot(p, q, preferred_element_type=f32)

    return dot(a_high, b_high) + (dot(a_low, b_high) + dot(a_high, b_low))


def merge_kernel(
    part, taps, weight, coadd, detection, recv, zpart, zrecv, mine, other, halo, rowk, colk, aid, sends, recvs, aid_sends, aid_recvs
):
    me, z, x, y = coords()
    band = lax.axis_index("band")
    above, below = (me + 127) % 128, (me + 1) % 128
    column = column_partners()
    sibling = {"patch": me, "band": 1 - band}
    near = [{"patch": p, "band": b} for p in (above, below) for b in (band, 1 - band)]
    greet(ring_partners() + column + [sibling] + near)

    def rows_of(c, lead):
        start = 0 if c == 0 else lead + c * CHUNK
        return pl.ds(start, lead + CHUNK if c == 0 else CHUNK)

    def ring_part(c):
        rows = rows_of(c, FAC)
        copies = ring_copies(
            lambda a, i: part.at[1 - a, i, pl.ds(0, 4), rows],
            lambda a, i: recv.at[1 - a, i, pl.ds(0, 4), rows],
            sends,
            recvs,
            6 * c,
        )
        for copy in copies:
            copy.start()
        return copies

    pending = [ring_part(0), ring_part(1)]
    wide = PATCH + 16
    row_gap = lax.broadcasted_iota(i32, (PATCH, wide), 1) - lax.broadcasted_iota(i32, (PATCH, wide), 0) - 4
    col_gap = lax.broadcasted_iota(i32, (PATCH, PATCH), 0) - lax.broadcasted_iota(i32, (PATCH, PATCH), 1) + 4
    row_kernel = jnp.zeros((PATCH, wide), f32)
    col_kernel = jnp.zeros((PATCH, PATCH), f32)
    for r in range(9):
        row_kernel = jnp.where(row_gap == r, taps[r], row_kernel)
        col_kernel = jnp.where(col_gap == r, taps[r], col_kernel)
    rowk[...] = row_kernel
    colk[...] = col_kernel

    zcopies, aids = [], []
    half = CHUNK // 2

    def z_copy(c, d, rows):
        to = (z + d) % NZ
        n = 6 * NCHUNK + 7 * c + d - 1
        copy = remote(zpart.at[to, rows], zrecv.at[z, rows], sends.at[n], recvs.at[n], to * 16 + x * 4 + y)
        copy.start()
        return copy

    def half_of(c, n):
        return pl.ds(4 * FAC + c * CHUNK + n * half, half)

    def aid_copy(c, n):
        near_z = (z + (1 if n == 0 else NZ - 1)) % NZ
        copy = remote(
            zpart.at[(z + 4) % NZ, half_of(c, n)],
            aid.at[c, n],
            aid_sends.at[2 * c + n],
            aid_recvs.at[2 * c + n],
            near_z * 16 + x * 4 + y,
        )
        copy.start()
        return copy

    def send_far(c):
        for n in range(2):
            aids[c][n].wait()
            d = 3 if n == 0 else 5
            to, rows = (z + d) % NZ, half_of(c, n)
            zpart[to, rows, :] = (zpart[to, rows, :].astype(f32) + aid[c, n].astype(f32)).astype(bf16)
            zcopies[c].append(z_copy(c, d, rows_of(c, 4 * FAC)))

    for c in range(NCHUNK):
        for copy in pending[c]:
            copy.wait()
        if c + 2 < NCHUNK:
            pending.append(ring_part(c + 2))
        for a in range(2):

            own = x if a else y

            def fold(zz, carry, a=a, c=c, own=own):
                if c == 0:
                    zpart[2 * zz + a, :FAC, :] = part[a, own, zz, :FAC, :]
                    for d in range(1, 4):
                        zpart[2 * zz + a, d * FAC : (d + 1) * FAC, :] = recv[a, (own + d) % 4, zz, :FAC, :]
                chunk = pl.ds(FAC + c * CHUNK, CHUNK)
                total = part[a, own, zz, chunk, :].astype(f32)
                for d in range(1, 4):
                    total = total + recv[a, (own + d) % 4, zz, chunk, :].astype(f32)
                at = 4 * FAC + c * CHUNK
                zpart[2 * zz + a, at : at + CHUNK, :] = total.astype(bf16)
                return carry

            lax.fori_loop(0, 4, fold, 0)
        zcopies.append([z_copy(c, d, rows_of(c, 4 * FAC)) for d in (2, 6, 1, 7)])
        if c == 0:
            zcopies[c].append(z_copy(c, 4, pl.ds(0, 4 * FAC)))
        aids.append([aid_copy(c, n) for n in range(2)])
        if c:
            send_far(c - 1)
    send_far(NCHUNK - 1)

    cover = None
    last = []
    base = 13 * NCHUNK
    for c in range(NCHUNK):
        for copy in zcopies[c]:
            copy.wait()
        if c == 0:
            row_sums, col_sums = [], []
            for d in range(NZ):
                sums = (zrecv[(z + d) % NZ, : 4 * FAC, :] if d else zpart[z, : 4 * FAC, :]).astype(f32)
                for q in range(4):
                    row_sums.append(sums[q * FAC : q * FAC + 8])
                    col_sums.append(sums[q * FAC + 8 : (q + 1) * FAC])
            cover = lax.dot_general(
                jnp.concatenate(row_sums, axis=0).astype(bf16),
                jnp.concatenate(col_sums, axis=0).astype(bf16),
                CONTRACT_FIRST,
                preferred_element_type=f32,
            )
            mine[...] = jnp.maximum(cover, 1.0)
        chunk = pl.ds(4 * FAC + c * CHUNK, CHUNK)
        total = zpart[z, chunk, :].astype(f32)
        for d in (1, 2, 3, 5, 6, 7):
            total = total + zrecv[(z + d) % NZ, chunk, :].astype(f32)
        rows = slice(c * CHUNK, (c + 1) * CHUNK)
        image = total / mine[rows, :]
        coadd[rows, :] = image
        mine[rows, :] = image * weight[0]
        ship = pl.ds(c * CHUNK, CHUNK)
        copies = [to_device(mine.at[ship], other.at[ship], sends.at[base + c], recvs.at[base + c], sibling)]
        if c == 0:
            for n in (0, 1):
                k = base + NCHUNK + n
                copies.append(to_device(mine.at[pl.ds(0, 8)], halo.at[1, n], sends.at[k], recvs.at[k], near[n]))
        if c == NCHUNK - 1:
            for n in (0, 1):
                k = base + NCHUNK + 2 + n
                copies.append(
                    to_device(mine.at[pl.ds(PATCH - 8, 8)], halo.at[0, n], sends.at[k], recvs.at[k], near[2 + n])
                )
        for copy in copies:
            copy.start()
        last += copies
    for copy in last:
        copy.wait()
    top = jnp.where(me == 0, 0.0, halo[0, 0] + halo[0, 1])
    bottom = jnp.where(me == 127, 0.0, halo[1, 0] + halo[1, 1])
    padded = jnp.concatenate([top, mine[...] + other[...], bottom], axis=0)
    row_pass = dot3(rowk[...], padded)
    detection[...] = dot3(row_pass, colk[...])


def merge(part, det_taps, band_weight):
    smem = pl.BlockSpec(memory_space=pltpu.SMEM)
    vmem = pl.BlockSpec(memory_space=pltpu.VMEM)
    image = jax.ShapeDtypeStruct((PATCH, PATCH), f32)
    count = 14 * NCHUNK + 4
    return pl.pallas_call(
        merge_kernel,
        out_shape=(image, image),
        in_specs=[vmem, smem, smem],
        out_specs=(vmem, vmem),
        scratch_shapes=[
            pltpu.VMEM((2, 4, 4, PROWS, PATCH), bf16),
            pltpu.VMEM((NZ, ZROWS, PATCH), bf16),
            pltpu.VMEM((NZ, ZROWS, PATCH), bf16),
            pltpu.VMEM((PATCH, PATCH), f32),
            pltpu.VMEM((PATCH, PATCH), f32),
            pltpu.VMEM((2, 2, 8, PATCH), f32),
            pltpu.VMEM((PATCH, PATCH + 16), f32),
            pltpu.VMEM((PATCH, PATCH), f32),
            pltpu.VMEM((NCHUNK, 2, CHUNK // 2, PATCH), bf16),
            pltpu.SemaphoreType.DMA((count,)),
            pltpu.SemaphoreType.DMA((count,)),
            pltpu.SemaphoreType.DMA((2 * NCHUNK,)),
            pltpu.SemaphoreType.DMA((2 * NCHUNK,)),
        ],
        compiler_params=pltpu.CompilerParams(collective_id=2, has_side_effects=True, vmem_limit_bytes=14 * MIB),
        name="merge",
    )(part.reshape(2, 4, 4, PROWS, PATCH), det_taps, band_weight)


def body(
    tiles, psf_coeff, row_taps, col_taps, target_patch, offsets, visits, warp_rows, warp_cols, det_taps, band_weight
):
    info = jnp.concatenate([target_patch[0].T, offsets[0].T, visits], axis=0)

    def widened(lines):
        return jnp.pad(lines, ((0, 16 - lines.shape[0]), (0, BW * TILE - lines.shape[1])))

    packed = [warp_rows[0], warp_cols[0], widened(psf_coeff[0].T), widened(row_taps), widened(col_taps)]
    slots, meta = match_tiles(info, jnp.concatenate(packed, axis=0), tiles[0].reshape(NTILE, TILE, TILE))
    recv, rmeta, most = route_tiles(slots, meta, CAP, 0)

    def few():
        return warp_tiles(rmeta, recv, slots, CAP)

    def many():
        whole, wmeta, _ = route_tiles(slots, meta, 32, 1)
        return warp_tiles(wmeta, whole, slots, 32)

    part = lax.cond(most[0, 3] > CAP, many, few)
    coadd, detection = merge(part, det_taps, band_weight)
    return coadd[None], detection


def solution(mesh):
    in_specs = (
        P("band", "patch", None),
        P("band", "patch", None),
        P(),
        P(),
        P("band", "patch", None),
        P("band", "patch", None),
        P("band", "patch"),
        P("band", "patch", None),
        P("band", "patch", None),
        P(),
        P("band"),
    )
    out_specs = (P("band", "patch", None), P("patch", None))
    return jax.shard_map(body, mesh=mesh, in_specs=in_specs, out_specs=out_specs, check_vma=False)
```
